256 devices in a mesh: gx: 4 (over z_hi), gy: 4 (over x), gz: 16 (over z_lo, y, core).
Axes of the slice: x: 4, y: 4, z: 8 (z_hi: 4, z_lo: 2; z = z_hi * 2 + z_lo), core: 2. Of those that a mesh axis runs over, the one named last changes fastest.
Arguments:
- vectors: bfloat16 [16, 64, 2048, 128], P('gx', 'gy', 'gz'), may hold values from -0.5 to 0.5
- diag_shift: float32 [2, 16, 64, 2048], P(None, 'gx', 'gy', 'gz'), may hold values from 0.5 to 2
- coupling: float32 [16, 64, 2048], P('gx', 'gy', 'gz'), may hold values from -0.4 to 0.4
- counts: int32 [256], P(('gx', 'gy', 'gz')), may hold values from 16 to 48, as said below
Outputs:
- coarse_rows: float32 [16384, 448], P(('gx', 'gy'))
- panel: float32 [16384, 512], P(('gx', 'gy', 'gz'))
The draws below stay inside these ranges and needn't reach their ends.
Inputs may be any that keep to these rules, and one draw needn't show every extreme that they name: `counts`: some subdomain uses 3 * 16 vectors and some uses 64 // 4.
All inputs are finite; a program needn't handle non-finite values.
Results may differ from the reference program's by a relative error of at most 0.0003.
Values may be sent and summed in bfloat16 or wider, within the bound.
A program may use at most 64 MiB of HBM per device.

```python
import jax
import jax.numpy as jnp
from jax import lax

CX = 4
CY = 16
CZ = 128
KS = 64
PANEL = 512
PSUB = 8
NX = 16
NY = 64
NZ = 2048
N_GX = 4
N_GY = 4
N_GZ = 16
DEVICES = 256


def draw_counts(key, part):
    key = jax.random.fold_in(key, 11)
    key_values, key_high, key_low = jax.random.split(key, 3)
    values = jax.random.randint(key_values, (DEVICES,), KS // 4, 3 * KS // 4 + 1, dtype=jnp.int32)
    high_at = jax.random.randint(key_high, (), 0, DEVICES, dtype=jnp.int32)
    low_at = (high_at + 1 + jax.random.randint(key_low, (), 0, DEVICES - 1, dtype=jnp.int32)) % DEVICES
    values = values.at[high_at].set(3 * KS // 4)
    values = values.at[low_at].set(KS // 4)
    return values


def draw_vectors(key, part):
    key = jax.random.fold_in(key, 7)
    key_noise, key_sign, key_size = jax.random.split(key, 3)
    shape = (NX, NY, NZ, 2 * KS)
    noise = 0.0625 * jax.random.normal(key_noise, shape, jnp.float32)
    lowest, highest, length = (0.4, 1.0, 2.0)
    lines = NZ // CZ
    signs = (2 * jax.random.randint(key_sign, (lines, 2 * KS), 0, 2, dtype=jnp.int32) - 1).astype(jnp.float32)
    sizes_drawn = jax.random.uniform(key_size, (lines, 2 * KS), jnp.float32, lowest, highest)
    amplitude = jnp.repeat(signs * sizes_drawn, CZ, axis=0)
    local = (jnp.arange(NZ, dtype=jnp.int32) % CZ).astype(jnp.float32)
    profile = jnp.exp(-local / length) + jnp.exp(-(CZ - 1.0 - local) / length)
    peak = 1.0 + jnp.exp(jnp.float32(-(CZ - 1.0) / length))
    coherent = 0.4 * (profile / peak)[:, None] * amplitude
    return jnp.clip(noise + coherent[None, None], -0.5, 0.5).astype(jnp.bfloat16)


def level_of(rng, extent, cuts, smallest, high):
    factor_of = 1.0
    for axis_at, parts in cuts:
        draws = jax.random.uniform(jax.random.fold_in(jax.random.fold_in(rng, 6), axis_at), (parts,), jnp.float32, smallest / len(cuts), high / len(cuts))
        factor_of = factor_of * jnp.repeat(jnp.exp(draws), extent[axis_at] // parts).reshape((-1,) + (1,) * (len(extent) - 1 - axis_at))
    return factor_of


def setup_inputs(seed: int = 0) -> dict:
    arg_keys = jax.random.split(jax.random.key(seed), 5)
    return {
        "vectors": draw_vectors(jax.random.fold_in(arg_keys[4], 71), 0),
        "diag_shift": jnp.clip(0.5 + 1.5 * jax.random.uniform(arg_keys[1], (2, NX, NY, NZ), jnp.float32) ** level_of(arg_keys[1], (2, NX, NY, NZ), ((1, 4), (2, 4), (3, 16)), -0.2, 0.2), 0.5, 2.0),
        "coupling": jnp.clip(jax.random.uniform(arg_keys[2], (NX, NY, NZ), jnp.float32, -0.4, 0.4) * level_of(arg_keys[2], (NX, NY, NZ), ((0, 4), (1, 4), (2, 16)), -0.4, 0.0), -0.4, 0.4),
        "counts": draw_counts(jax.random.fold_in(arg_keys[4], 71), 0),
    }


def live_mask(count, slots):
    return (jnp.arange(slots, dtype=jnp.int32) < count).astype(jnp.float32)

def apply_operator(field, shift, coupling):
    half = field.shape[-1] // 2
    padded = jnp.pad(field, ((1, 1), (1, 1), (1, 1), (0, 0)))
    beside = padded[2:, 1:-1, 1:-1] + padded[:-2, 1:-1, 1:-1]
    beside = beside + padded[1:-1, 2:, 1:-1] + padded[1:-1, :-2, 1:-1]
    beside = beside + padded[1:-1, 1:-1, 2:] + padded[1:-1, 1:-1, :-2]
    first = field[..., :half]
    second = field[..., half:]
    out_first = (6.0 + shift[0])[..., None] * first + coupling[..., None] * second - beside[..., :half]
    out_second = (6.0 + shift[1])[..., None] * second + coupling[..., None] * first - beside[..., half:]
    return jnp.concatenate([out_first, out_second], axis=-1)

def pair_block(own, other):
    slots = own.shape[-1] // 2
    left = own.astype(jnp.float32).reshape(-1, 2, slots)
    right = other.astype(jnp.float32).reshape(-1, 2, slots)
    return -jnp.einsum('nck,ncl->kl', left, right, precision=lax.Precision.HIGHEST)

def self_block(masked, shift, coupling, live):
    slots = masked.shape[-1] // 2
    field = masked.astype(jnp.float32)
    image = apply_operator(field, shift, coupling)
    gram = jnp.einsum('nck,ncl->kl', field.reshape(-1, 2, slots), image.reshape(-1, 2, slots), precision=lax.Precision.HIGHEST)
    return gram + jnp.diag(1.0 - live)

def reference(vectors, diag_shift, coupling, counts):
    step_x = N_GY * N_GZ
    zero = jnp.int32(0)

    def subdomain(linear):
        ia = linear // step_x
        ib = linear // N_GZ % N_GY
        ic = linear % N_GZ
        ox = (ia * CX).astype(jnp.int32)
        oy = (ib * CY).astype(jnp.int32)
        oz = (ic * CZ).astype(jnp.int32)
        live = live_mask(counts[linear], KS)

        def masked_at(start, shape, weight):
            piece = lax.dynamic_slice(vectors, start, shape)
            return piece * jnp.concatenate([weight, weight]).astype(jnp.bfloat16)

        def neighbour_face(start, shape, index, valid):
            index = jnp.clip(index, 0, DEVICES - 1).astype(jnp.int32)
            weight = live_mask(counts[index], KS) * valid.astype(jnp.float32)
            return masked_at(start, shape, weight)
        own = masked_at((ox, oy, oz, zero), (CX, CY, CZ, 2 * KS), live)
        shift = lax.dynamic_slice(diag_shift, (zero, ox, oy, oz), (2, CX, CY, CZ))
        coup = lax.dynamic_slice(coupling, (ox, oy, oz), (CX, CY, CZ))
        center = self_block(own, shift, coup, live)
        face_xm = neighbour_face((jnp.maximum(ox - 1, 0).astype(jnp.int32), oy, oz, zero), (1, CY, CZ, 2 * KS), linear - step_x, ia > 0)[0]
        face_xp = neighbour_face((jnp.minimum(ox + CX, NX - 1).astype(jnp.int32), oy, oz, zero), (1, CY, CZ, 2 * KS), linear + step_x, ia < N_GX - 1)[0]
        face_ym = neighbour_face((ox, jnp.maximum(oy - 1, 0).astype(jnp.int32), oz, zero), (CX, 1, CZ, 2 * KS), linear - N_GZ, ib > 0)[:, 0]
        face_yp = neighbour_face((ox, jnp.minimum(oy + CY, NY - 1).astype(jnp.int32), oz, zero), (CX, 1, CZ, 2 * KS), linear + N_GZ, ib < N_GY - 1)[:, 0]
        face_zm = neighbour_face((ox, oy, jnp.maximum(oz - 1, 0).astype(jnp.int32), zero), (CX, CY, 1, 2 * KS), linear - 1, ic > 0)[:, :, 0]
        face_zp = neighbour_face((ox, oy, jnp.minimum(oz + CZ, NZ - 1).astype(jnp.int32), zero), (CX, CY, 1, 2 * KS), linear + 1, ic < N_GZ - 1)[:, :, 0]
        return jnp.stack([center, pair_block(own[0], face_xm), pair_block(own[-1], face_xp), pair_block(own[:, 0], face_ym), pair_block(own[:, -1], face_yp), pair_block(own[:, :, 0], face_zm), pair_block(own[:, :, -1], face_zp)])
    linears = jnp.arange(DEVICES, dtype=jnp.int32)
    all_blocks = lax.map(subdomain, linears)
    coarse_rows = jnp.transpose(all_blocks, (0, 2, 1, 3)).reshape(DEVICES * KS, 7 * KS)
    neighbours = jnp.stack([linears, linears - step_x, linears + step_x, linears - N_GZ, linears + N_GZ, linears - 1, linears + 1], axis=1)
    select = (neighbours[:, :, None] == jnp.arange(PSUB, dtype=jnp.int32)[None, None, :]).astype(jnp.float32)
    panel_rows = jnp.einsum('dbj,dbkl->dkjl', select, all_blocks, precision=lax.Precision.HIGHEST).reshape(DEVICES * KS, PANEL)
    leading = panel_rows[:PANEL]
    factor = jnp.linalg.cholesky(leading)
    panel = lax.linalg.triangular_solve(factor, panel_rows, left_side=False, lower=True, transpose_a=True)
    return (coarse_rows, panel)
```

```python
import functools

import jax
import jax.numpy as jnp
from jax import lax
from jax.experimental import pallas as pl
from jax.experimental.pallas import tpu as pltpu
from jax.sharding import PartitionSpec as P

F = jnp.float32
BF = jnp.bfloat16
CX, CY, CZ = 4, 16, 128
KS = 64
KL = 48
PSUB = 8
NGX, NGY, NGZ = 4, 4, 16
GROUP = 16
MESH = pl.DeviceIdType.MESH


def remote(src, dst, send, recv, device):
    return pltpu.make_async_remote_copy(
        src_ref=src, dst_ref=dst, send_sem=send, recv_sem=recv, device_id=device, device_id_type=MESH
    )


def lanes_of(x, c):
    return jnp.broadcast_to(x[:, c : c + 1], (8, 128))


def rows_of(x, r):
    return jnp.broadcast_to(x[r : r + 1, :], (8, 128))


def eliminate(A):
    rows = lax.broadcasted_iota(jnp.int32, (8, 128), 0)
    n = KL // 8
    for first in range(0, KL, GROUP):
        copies = [[None] * n for _ in range(GROUP)]
        for c in range(GROUP):
            for i in range(first // 8, n):
                copies[c][i] = lanes_of(A[i][0], first + c)
        for c in range(GROUP):
            J, s = (first + c) // 8, c % 8
            r = lax.rsqrt(rows_of(copies[c][J], s))
            row = [rows_of(a, s) * r for a in A[J]]
            beside = [rows_of(copies[k][J], s) * r for k in range(c + 1, GROUP)]
            for i in range(J, n):
                f = copies[c][i] * r
                if i == J:
                    f = jnp.where(rows > s, f, 0.0)
                for q in range(len(row)):
                    A[i][q] = A[i][q] - f * row[q]
                for k in range(c + 1, GROUP):
                    copies[k][i] = copies[k][i] - f * beside[k - c - 1]
            for q in range(len(row)):
                A[J][q] = jnp.where(rows == s, row[q], A[J][q])
    return A


def split3(x):
    h = x.astype(BF)
    x = x - h.astype(F)
    m = x.astype(BF)
    x = x - m.astype(F)
    return h, m, x.astype(BF)


TN = (((0,), (0,)), ((), ()))


def outer_gram(M):
    h, m, low = split3(M)
    left1 = jnp.concatenate([h[:, :KS], h[:, :KS], m[:, :KS]], 0)
    right1 = jnp.concatenate([h, m, h], 0)
    left2 = jnp.concatenate([m[:, :KS], h[:, :KS], low[:, :KS]], 0)
    right2 = jnp.concatenate([m, low, h], 0)
    return lax.dot_general(left1, right1, TN, preferred_element_type=F) + lax.dot_general(
        left2, right2, TN, preferred_element_type=F
    )


def kernel(
    cnt_ref, m_hbm, s_hbm, c_hbm, rows_out, panel_ref,
    m, tt, sh, cp, yb, xr, yr, zs, zr, part, partr, lead, rhs, xs, sub, row, const,
    load, xsend, xrecv, ysend, yrecv, zsend, zrecv, psend, precv, lsend, lrecv, rsend, rrecv, csem,
):
    gx, gy, gz = lax.axis_index("gx"), lax.axis_index("gy"), lax.axis_index("gz")
    has = {
        "xm": gx > 0, "xp": gx < NGX - 1,
        "ym": gy > 0, "yp": gy < NGY - 1,
        "zm": gz > 0, "zp": gz < NGZ - 1,
    }
    beside = {
        "xm": {"gx": gx - 1}, "xp": {"gx": gx + 1},
        "ym": {"gy": gy - 1}, "yp": {"gy": gy + 1},
        "zm": {"gz": gz - 1}, "zp": {"gz": gz + 1},
    }
    fetch = [pltpu.make_async_copy(m_hbm.at[x], m.at[x], load.at[x]) for x in range(CX)]
    fetch_s = pltpu.make_async_copy(s_hbm, sh, load.at[4])
    fetch_c = pltpu.make_async_copy(c_hbm, cp, load.at[5])
    for x in (3, 0, 1, 2):
        fetch[x].start()
    fetch_s.start()
    fetch_c.start()

    barrier = pltpu.get_barrier_semaphore()
    for k in range(1, NGZ):
        pl.semaphore_signal(barrier, inc=1, device_id={"gz": lax.rem(gz + k, NGZ)}, device_id_type=MESH)
    for side in ("xm", "xp", "ym", "yp"):
        @pl.when(has[side])
        def _():
            pl.semaphore_signal(barrier, inc=1, device_id=beside[side], device_id_type=MESH)

    r16 = lax.broadcasted_iota(jnp.int32, (16, 7 * KS), 0)
    l16 = lax.broadcasted_iota(jnp.int32, (16, 7 * KS), 1)
    const[...] = jnp.where(l16 == r16 + KL, 1.0, 0.0)
    fills = [
        pltpu.make_async_copy(const, rows_out.at[pl.ds(KS * t + KL, KS - KL), :], csem.at[t]) for t in range(NGZ)
    ]
    for f in fills:
        f.start()

    count = cnt_ref[0]
    r128 = lax.broadcasted_iota(jnp.int32, (128, 128), 0)
    l128 = lax.broadcasted_iota(jnp.int32, (128, 128), 1)
    live_rows = (jnp.where(r128 >= KS, r128 - KS, r128) < count).astype(F).astype(BF)
    live_lanes = (jnp.where(l128 >= KS, l128 - KS, l128) < count)[:KS]

    def transpose(x):
        def body(y, _):
            t = jnp.swapaxes(m[x, y], 0, 1) * live_rows
            tt[x, y, 0:KL] = t[0:KL]
            tt[x, y, KL : 2 * KL] = t[KS : KS + KL]
            return 0

        lax.fori_loop(0, CY, body, 0, unroll=4)

    fetch[3].wait()
    transpose(3)
    fetch[0].wait()
    transpose(0)
    peers = sum(has[side].astype(jnp.int32) for side in ("xm", "xp", "ym", "yp"))
    pl.semaphore_wait(barrier, NGZ - 1 + peers)

    half = CY // 2
    x_up = remote(tt.at[3, pl.ds(0, half)], xr.at[0], xsend.at[0], xrecv.at[0], beside["xp"])
    x_down = remote(tt.at[0, pl.ds(half, half)], xr.at[1], xsend.at[1], xrecv.at[1], beside["xm"])
    y_up = remote(tt.at[:, CY - 1], yr.at[0], ysend.at[0], yrecv.at[0], beside["yp"])
    y_down = remote(tt.at[:, 0], yr.at[1], ysend.at[1], yrecv.at[1], beside["ym"])
    z_up = remote(zs.at[1], zr.at[0], zsend.at[0], zrecv.at[0], beside["zp"])
    z_down = remote(zs.at[0], zr.at[1], zsend.at[1], zrecv.at[1], beside["zm"])
    p_up = remote(part.at[1], partr.at[0], psend.at[0], precv.at[0], beside["xp"])
    p_down = remote(part.at[0], partr.at[1], psend.at[1], precv.at[1], beside["xm"])
    ways = [
        ("xp", x_up), ("xm", x_down), ("yp", y_up), ("ym", y_down),
        ("zp", z_up), ("zm", z_down), ("xp", p_up), ("xm", p_down),
    ]

    def start(side, copy):
        @pl.when(has[side])
        def _():
            copy.start()

    def arrived(side, copy, buffer, slot):
        @pl.when(has[side])
        def _():
            copy.wait_recv()

        @pl.when(jnp.logical_not(has[side]))
        def _():
            buffer[slot] = jnp.zeros(buffer.shape[1:], buffer.dtype)

    start("xp", x_up)
    start("xm", x_down)

    fetch[1].wait()
    fetch[2].wait()
    for x in range(CX):
        low = m[x, :, 0:16, :].astype(F)[:, 0, :]
        high = m[x, :, CZ - 16 : CZ, :].astype(F)[:, 15, :]
        ok = live_lanes[:CY]
        zs[0, CY * x : CY * (x + 1)] = jnp.where(ok, low, 0.0).astype(BF)
        zs[1, CY * x : CY * (x + 1)] = jnp.where(ok, high, 0.0).astype(BF)
    start("zp", z_up)
    start("zm", z_down)
    transpose(1)
    transpose(2)
    start("yp", y_up)
    start("ym", y_down)

    fetch_s.wait()
    fetch_c.wait()
    lane = lax.broadcasted_iota(jnp.int32, (KL, 128), 1)
    inner_z = jnp.where(lane < CZ - 1, 1.0, 0.0)
    G = jnp.zeros((4 * KL, 128), F)
    for x in range(CX):
        def body(y, _):
            wide = (KL, 128)
            a0 = jnp.broadcast_to(sh[0, x, pl.ds(y, 1), :] + 6.0, wide)
            a1 = jnp.broadcast_to(sh[1, x, pl.ds(y, 1), :] + 6.0, wide)
            c = jnp.broadcast_to(cp[x, pl.ds(y, 1), :], wide)
            u = tt[x, y, 0:KL, :].astype(F)
            v = tt[x, y, KL : 2 * KL, :].astype(F)
            y2 = jnp.minimum(y + 1, CY - 1)
            inner_y = jnp.where(y < CY - 1, 1.0, 0.0).astype(F)

            def forward(w, at):
                n = pltpu.roll(w, CZ - 1, 1) * inner_z
                n = n + tt[x, y2, at : at + KL, :].astype(F) * inner_y
                if x < CX - 1:
                    n = n + tt[x + 1, y, at : at + KL, :].astype(F)
                return n

            yu = a0 * u + c * v - 2.0 * forward(u, 0)
            yv = a1 * v + c * u - 2.0 * forward(v, KL)
            at = pl.ds(pl.multiple_of(y * 128, 128), 128)
            for k, w in enumerate((yu, yv)):
                h = w.astype(BF)
                yb[KL * k : KL * (k + 1), at] = h
                yb[KL * (2 + k) : KL * (3 + k), at] = (w - h.astype(F)).astype(BF)
            return 0

        lax.fori_loop(0, CY, body, 0, unroll=2)
        G = G + jnp.dot(yb[...], m[x].reshape(CY * CZ, 128), preferred_element_type=F)
    G = G[: 2 * KL] + G[2 * KL :]

    def both(g):
        return jnp.where(live_lanes[:KL, :KS], g[:KL, :KS] + g[KL : 2 * KL, KS:], 0.0)

    def flip(b):
        wide = jnp.concatenate([b, jnp.zeros((KL, KS), F)], 1)
        wide = jnp.concatenate([wide, jnp.zeros((128 - KL, 128), F)], 0)
        return jnp.transpose(wide)[:KL, :KS]

    C = both(G)
    C = 0.5 * (C + flip(C))
    r48 = lax.broadcasted_iota(jnp.int32, (KL, KS), 0)
    l48 = lax.broadcasted_iota(jnp.int32, (KL, KS), 1)
    C = jnp.where((r48 == l48) & (r48 >= count), 1.0, C)

    def both_z(g):
        return -(g[:KL, :KS] + g[KS : KS + KL, KS:])

    arrived("zm", z_up, zr, 0)
    arrived("zp", z_down, zr, 1)
    zp = both_z(lax.dot_general(zs[1], zr[1], TN, preferred_element_type=F))

    line0 = (gx == 0) & (gy == 0)
    line_y = (gx == 0) & (gy == 1)
    line_x = (gx == 1) & (gy == 0)
    lines = line0 | line_y | line_x
    source = lines & (gz < PSUB)
    chained = lines & (gz <= PSUB)
    slot = jnp.minimum(gz, PSUB - 1)
    mine = lead.at[slot]
    to_y = remote(mine, mine, lsend.at[PSUB + 1], lrecv.at[slot], beside["yp"])
    to_x = remote(mine, mine, lsend.at[PSUB + 2], lrecv.at[slot], beside["xp"])
    along = [remote(mine, mine, lsend.at[t], lrecv.at[slot], {"gz": t}) for t in range(PSUB + 1)]

    @pl.when(line0 & (gz < PSUB))
    def _():
        lead[slot] = jnp.concatenate([C, zp], 1)
        to_y.start()
        to_x.start()

    @pl.when((line_y | line_x) & (gz < PSUB))
    def _():
        to_y.wait_recv()

    for t in range(PSUB + 1):
        @pl.when(source & (gz != t))
        def _():
            along[t].start()

    zmT = both_z(lax.dot_general(zr[0], zs[0], TN, preferred_element_type=F))
    zpT = both_z(lax.dot_general(zr[1], zs[1], TN, preferred_element_type=F))
    zm = both_z(lax.dot_general(zs[0], zr[0], TN, preferred_element_type=F))

    def face(tiles, own):
        left = jnp.concatenate(tiles, 1)
        right = jnp.concatenate(own, 0)
        return -both(jnp.dot(left, right, preferred_element_type=F))

    arrived("ym", y_up, yr, 0)
    arrived("yp", y_down, yr, 1)
    ymT = face([yr[0, x] for x in range(CX)], [m[x, 0] for x in range(CX)])
    ypT = face([yr[1, x] for x in range(CX)], [m[x, CY - 1] for x in range(CX)])
    ym, yp = flip(ymT), flip(ypT)
    arrived("xm", x_up, xr, 0)
    arrived("xp", x_down, xr, 1)
    low = face([xr[0, y] for y in range(half)], [m[0, y] for y in range(half)])
    high = face([xr[1, y] for y in range(half)], [m[CX - 1, half + y] for y in range(half)])
    part[0] = jnp.concatenate([flip(low), jnp.zeros((KL, KS), F)], 1)
    part[1] = jnp.concatenate([flip(high), jnp.zeros((KL, KS), F)], 1)
    start("xp", p_up)
    start("xm", p_down)
    arrived("xm", p_up, partr, 0)
    arrived("xp", p_down, partr, 1)
    xmT = low + partr[0, :, :KS]
    xpT = high + partr[1, :, :KS]
    xm, xp = flip(xmT), flip(xpT)
    row[...] = jnp.concatenate([C, xm, xp, ym, yp, zm, zp], 1)

    partner = lax.rem(gz + 8, NGZ)
    sibling = gz + 1 - 2 * lax.rem(gz, 2)
    plane = 8 * (gz // 8)
    in_plane = gz - plane
    around = [plane + lax.rem(in_plane + 2 * k, 8) for k in range(1, 4)]
    around_partner = [lax.rem(a + 8, NGZ) for a in around]

    def at_row(c):
        return rows_out.at[pl.ds(pl.multiple_of(KS * c, KS), KL), :]

    def give(c, target, k):
        src = row if c is gz else at_row(c)
        return remote(src, at_row(c), rsend.at[k], rrecv.at[c], {"gz": target})

    def wait_row(c):
        remote(at_row(c), at_row(c), rsend.at[0], rrecv.at[c], {"gz": partner}).wait_recv()

    sends = [give(gz, partner, 0), give(gz, sibling, 1)] + [give(gz, a, 2 + k) for k, a in enumerate(around)]
    sends_b = [give(partner, a, 5 + k) for k, a in enumerate(around)] + [give(partner, sibling, 8)]
    sends_c = [give(a, sibling, 9 + k) for k, a in enumerate(around)]
    sends_d = [give(a, sibling, 12 + k) for k, a in enumerate(around_partner)]
    own = pltpu.make_async_copy(row, at_row(gz), load.at[6])
    own.start()
    for s in sends:
        s.start()

    zero = jnp.zeros((KL, KS), F)
    for i in range(PSUB):
        b = jnp.where(line0 & (gz == i), C, zero)
        b = jnp.where(line0 & (gz == i - 1), zpT, b)
        b = jnp.where(line0 & (gz == i + 1), zmT, b)
        b = jnp.where(line_y & (gz == i), ymT, b)
        b = jnp.where(line_x & (gz == i), xmT, b)
        rhs[i] = b
        xs[i] = zero
    sub[...] = jnp.zeros((KL, 128), F)

    for t in range(PSUB):
        @pl.when(chained & jnp.logical_not(source & (gz == t)))
        def _():
            remote(lead.at[t], lead.at[t], lsend.at[0], lrecv.at[t], beside["zp"]).wait_recv()

    def step(i, _):
        pad = jnp.zeros((KL, KS), F)
        g = sub[...]
        a1 = lead[i] - jnp.concatenate([g[:, :KS], pad], 1)
        a2 = jnp.concatenate([rhs[i] - g[:, KS:], pad], 1)
        A = eliminate([[a1[8 * k : 8 * k + 8], a2[8 * k : 8 * k + 8]] for k in range(KL // 8)])
        a1 = jnp.concatenate([a[0] for a in A], 0)
        a2 = jnp.concatenate([a[1] for a in A], 0)
        xs[i] = a2[:, :KS]
        sub[...] = outer_gram(jnp.concatenate([a1[:, KS:], a2[:, :KS]], 1))[:KL]
        return 0

    def chain(low, high):
        @pl.when(chained)
        def _():
            lax.fori_loop(low, high, step, 0)

    chain(0, 2)
    wait_row(partner)
    for s in sends_b:
        s.start()
    chain(2, 5)
    for a in around:
        wait_row(a)
    for s in sends_c:
        s.start()
    for a in around_partner:
        wait_row(a)
    for s in sends_d:
        s.start()
    chain(5, PSUB)

    r64 = lax.broadcasted_iota(jnp.int32, (KS, KS), 0)
    l64 = lax.broadcasted_iota(jnp.int32, (KS, KS), 1)
    dead = jnp.where((r64 == l64) & (r64 >= KL), 1.0, 0.0)
    for p in range(PSUB // 2):
        tops = jnp.concatenate([xs[2 * p], jnp.zeros((KS - KL, KS), F), xs[2 * p + 1], jnp.zeros((KS - KL, KS), F)], 0)
        tops = jnp.concatenate([tops, jnp.zeros((128, KS), F)], 1)
        ends = jnp.concatenate(
            [jnp.where(line0 & (gz == 2 * p + k), dead, jnp.zeros((KS, KS), F)) for k in range(2)], 1
        )
        panel_ref[:, 128 * p : 128 * (p + 1)] = jnp.transpose(tops)[:KS] + ends

    wait_row(sibling)
    for a in [partner] + around + around_partner:
        wait_row(a + 1 - 2 * lax.rem(a, 2))
    own.wait()
    for f in fills:
        f.wait()
    for s in sends + sends_b + sends_c + sends_d:
        s.wait_send()
    for side, copy in ways:
        @pl.when(has[side])
        def _():
            copy.wait_send()

    @pl.when(line0 & (gz < PSUB))
    def _():
        to_y.wait_send()
        to_x.wait_send()

    for t in range(PSUB + 1):
        @pl.when(source & (gz != t))
        def _():
            along[t].wait_send()


def local(vectors, diag_shift, coupling, counts):
    dma = pltpu.SemaphoreType.DMA
    return pl.pallas_call(
        kernel,
        out_shape=(
            jax.ShapeDtypeStruct((NGZ * KS, 7 * KS), F),
            jax.ShapeDtypeStruct((KS, PSUB * KS), F),
        ),
        in_specs=[pl.BlockSpec(memory_space=pltpu.SMEM)] + [pl.BlockSpec(memory_space=pl.ANY)] * 3,
        out_specs=(pl.BlockSpec(memory_space=pl.ANY), pl.BlockSpec(memory_space=pltpu.VMEM)),
        scratch_shapes=[
            pltpu.VMEM((CX, CY, CZ, 128), BF),
            pltpu.VMEM((CX, CY, 2 * KL, CZ), BF),
            pltpu.VMEM((2, CX, CY, CZ), F),
            pltpu.VMEM((CX, CY, CZ), F),
            pltpu.VMEM((4 * KL, CY * CZ), BF),
            pltpu.VMEM((2, CY // 2, 2 * KL, CZ), BF),
            pltpu.VMEM((2, CX, 2 * KL, CZ), BF),
            pltpu.VMEM((2, CX * CY, 128), BF),
            pltpu.VMEM((2, CX * CY, 128), BF),
            pltpu.VMEM((2, KL, 128), F),
            pltpu.VMEM((2, KL, 128), F),
            pltpu.VMEM((PSUB, KL, 128), F),
            pltpu.VMEM((PSUB, KL, KS), F),
            pltpu.VMEM((PSUB, KL, KS), F),
            pltpu.VMEM((KL, 128), F),
            pltpu.VMEM((KL, 7 * KS), F),
            pltpu.VMEM((KS - KL, 7 * KS), F),
            dma((7,)),
            dma((2,)), dma((2,)), dma((2,)), dma((2,)), dma((2,)), dma((2,)), dma((2,)), dma((2,)),
            dma((PSUB + 3,)), dma((PSUB,)), dma((15,)), dma((NGZ,)), dma((NGZ,)),
        ],
        compiler_params=pltpu.CompilerParams(
            collective_id=0, has_side_effects=True, vmem_limit_bytes=40 << 20
        ),
    )(counts, vectors, diag_shift, coupling)


def solution(mesh):
    return jax.shard_map(
        local,
        mesh=mesh,
        in_specs=(
            P("gx", "gy", "gz", None),
            P(None, "gx", "gy", "gz"),
            P("gx", "gy", "gz"),
            P(("gx", "gy", "gz")),
        ),
        out_specs=(P(("gx", "gy"), None), P(("gx", "gy", "gz"), None)),
        check_vma=False,
    )
```

```python
import jax
import jax.numpy as jnp
from jax import lax
from jax.experimental import pallas as pl
from jax.experimental.pallas import tpu as pltpu
from jax.sharding import PartitionSpec as P

F = jnp.float32
BF = jnp.bfloat16
CX, CY, CZ = 4, 16, 128
KS = 64
KL = 48
PSUB = 8
NGX, NGY, NGZ = 4, 4, 16
GROUP = 16
MESH = pl.DeviceIdType.MESH


def remote(src, dst, send, recv, device):
    return pltpu.make_async_remote_copy(
        src_ref=src, dst_ref=dst, send_sem=send, recv_sem=recv, device_id=device, device_id_type=MESH
    )


def lanes_of(x, c):
    return jnp.broadcast_to(x[:, c : c + 1], (8, 128))


def rows_of(x, r):
    return jnp.broadcast_to(x[r : r + 1, :], (8, 128))


def eliminate(A):
    rows = lax.broadcasted_iota(jnp.int32, (8, 128), 0)
    n = KL // 8
    for first in range(0, KL, GROUP):
        copies = [[None] * n for _ in range(GROUP)]
        for c in range(GROUP):
            for i in range(first // 8, n):
                copies[c][i] = lanes_of(A[i][0], first + c)
        p = rows_of(copies[0][first // 8], 0)
        for c in range(GROUP):
            J, s = (first + c) // 8, c % 8
            if c + 1 < GROUP:
                ahead = rows_of(copies[c + 1][(first + c + 1) // 8], (c + 1) % 8)
            r = lax.rsqrt(p)
            row = [rows_of(a, s) * r for a in A[J]]
            beside = [rows_of(copies[k][J], s) * r for k in range(c + 1, GROUP)]
            if c + 1 < GROUP:
                p = ahead - beside[0] * beside[0]
            for i in range(J, n):
                f = copies[c][i] * r
                if i == J:
                    f = jnp.where(rows > s, f, 0.0)
                for q in range(len(row)):
                    A[i][q] = A[i][q] - f * row[q]
                for k in range(c + 1, GROUP):
                    copies[k][i] = copies[k][i] - f * beside[k - c - 1]
            for q in range(len(row)):
                A[J][q] = jnp.where(rows == s, row[q], A[J][q])
    return A


def split3(x):
    h = x.astype(BF)
    x = x - h.astype(F)
    m = x.astype(BF)
    x = x - m.astype(F)
    return h, m, x.astype(BF)


TN = (((0,), (0,)), ((), ()))


def outer_gram(M):
    h, m, low = split3(M)
    left1 = jnp.concatenate([h[:, :KS], h[:, :KS], m[:, :KS]], 0)
    right1 = jnp.concatenate([h, m, h], 0)
    left2 = jnp.concatenate([m[:, :KS], h[:, :KS], low[:, :KS]], 0)
    right2 = jnp.concatenate([m, low, h], 0)
    return lax.dot_general(left1, right1, TN, preferred_element_type=F) + lax.dot_general(
        left2, right2, TN, preferred_element_type=F
    )


def kernel(
    cnt_ref, m_hbm, s_hbm, c_hbm, out, panel_ref,
    m, tt, sh, cp, xr, yr, zs, zr, part, partr, lead, rhs, xs, sub, gath,
    load, xsend, xrecv, ysend, yrecv, zsend, zrecv, psend, precv, lsend, lrecv, esend, erecv, rsend, rrecv,
):
    gx, gy, gz = lax.axis_index("gx"), lax.axis_index("gy"), lax.axis_index("gz")
    has = {
        "xm": gx > 0, "xp": gx < NGX - 1,
        "ym": gy > 0, "yp": gy < NGY - 1,
        "zm": gz > 0, "zp": gz < NGZ - 1,
    }
    beside = {
        "xm": {"gx": gx - 1}, "xp": {"gx": gx + 1},
        "ym": {"gy": gy - 1}, "yp": {"gy": gy + 1},
        "zm": {"gz": gz - 1}, "zp": {"gz": gz + 1},
    }
    half = CY // 2
    fetch = {}
    for k, (x, h) in enumerate([(3, 0), (0, 1), (3, 1), (0, 0), (2, None), (1, None)]):
        part_of = (x,) if h is None else (x, pl.ds(half * h, half))
        fetch[x, h] = pltpu.make_async_copy(m_hbm.at[part_of], m.at[part_of], load.at[k])
        fetch[x, h].start()
    fetch_s = pltpu.make_async_copy(s_hbm, sh, load.at[6])
    fetch_c = pltpu.make_async_copy(c_hbm, cp, load.at[7])
    fetch_s.start()
    fetch_c.start()

    barrier = pltpu.get_barrier_semaphore()
    core = lax.rem(gz, 2)
    partner = lax.rem(gz + 8, NGZ)
    sibling = gz + 1 - 2 * core
    plane = 8 * (gz // 8)
    ring = lambda k: plane + lax.rem(gz - plane + 2 * k, 8)
    up, opposite, down = ring(1), ring(2), ring(3)
    line0 = (gx == 0) & (gy == 0)
    line_y = (gx == 0) & (gy == 1)
    line_x = (gx == 1) & (gy == 0)
    leader = line0 & (gz < PSUB)
    chained = (line0 & (gz <= PSUB)) | ((line_y | line_x) & (gz < PSUB))

    also = lambda c: lax.rem(c + 8, NGZ)
    around = (up, down, opposite)
    for t in (partner, sibling) + around + tuple(also(t) for t in around):
        pl.semaphore_signal(barrier, inc=1, device_id={"gz": t}, device_id_type=MESH)
    peers = 8
    for side in has:
        @pl.when(has[side])
        def _():
            pl.semaphore_signal(barrier, inc=1, device_id=beside[side], device_id_type=MESH)

        peers = peers + has[side].astype(jnp.int32)
    for t in range(PSUB):
        @pl.when(chained & jnp.logical_not(line0 & (gz == t)))
        def _():
            pl.semaphore_signal(barrier, inc=1, device_id={"gx": 0, "gy": 0, "gz": t}, device_id_type=MESH)
    peers = peers + jnp.where(leader, 3 * PSUB, 0)

    count = cnt_ref[0]
    r128 = lax.broadcasted_iota(jnp.int32, (128, 128), 0)
    l128 = lax.broadcasted_iota(jnp.int32, (128, 128), 1)
    live_rows = (jnp.where(r128 >= KS, r128 - KS, r128) < count).astype(F).astype(BF)
    live_lanes = (jnp.where(l128 >= KS, l128 - KS, l128) < count)[:KS]

    inner_z = jnp.where(lax.broadcasted_iota(jnp.int32, (KL, 128), 1) < CZ - 1, 1.0, 0.0)

    def transpose(x, y):
        t = jnp.swapaxes(m[x, y], 0, 1) * live_rows
        tt[x, y, 0:KL] = t[0:KL]
        tt[x, y, KL : 2 * KL] = t[KS : KS + KL]

    def image(x, y):
        wide = (KL, 128)
        a0 = jnp.broadcast_to(sh[0, x, y : y + 1, :] + 6.0, wide)
        a1 = jnp.broadcast_to(sh[1, x, y : y + 1, :] + 6.0, wide)
        c = jnp.broadcast_to(cp[x, y : y + 1, :], wide)
        u = tt[x, y, 0:KL, :].astype(F)
        v = tt[x, y, KL : 2 * KL, :].astype(F)

        def forward(w, at):
            n = pltpu.roll(w, CZ - 1, 1) * inner_z
            if y < CY - 1:
                n = n + tt[x, y + 1, at : at + KL, :].astype(F)
            if x < CX - 1:
                n = n + tt[x + 1, y, at : at + KL, :].astype(F)
            return n

        yu = a0 * u + c * v - 2.0 * forward(u, 0)
        yv = a1 * v + c * u - 2.0 * forward(v, KL)
        high = [w.astype(BF) for w in (yu, yv)]
        return jnp.concatenate(high + [(w - h.astype(F)).astype(BF) for w, h in zip((yu, yv), high)], 0)

    def stage(tx, yx, G, ys=range(0, CY, 2)):
        for y in ys:
            if tx is not None:
                transpose(tx, y)
                transpose(tx, y + 1)
            if yx is not None:
                left = jnp.concatenate([image(yx, y), image(yx, y + 1)], 1)
                right = jnp.concatenate([m[yx, y], m[yx, y + 1]], 0)
                G = G + jnp.dot(left, right, preferred_element_type=F)
        return G

    x_up = remote(tt.at[3, pl.ds(0, half)], xr.at[0], xsend.at[0], xrecv.at[0], beside["xp"])
    x_down = remote(tt.at[0, pl.ds(half, half)], xr.at[1], xsend.at[1], xrecv.at[1], beside["xm"])
    y_up = remote(tt.at[:, CY - 1], yr.at[0], ysend.at[0], yrecv.at[0], beside["yp"])
    y_down = remote(tt.at[:, 0], yr.at[1], ysend.at[1], yrecv.at[1], beside["ym"])
    z_up = remote(zs.at[1], zr.at[0], zsend.at[0], zrecv.at[0], beside["zp"])
    z_down = remote(zs.at[0], zr.at[1], zsend.at[1], zrecv.at[1], beside["zm"])
    p_up = remote(part.at[1], partr.at[0], psend.at[0], precv.at[0], beside["xp"])
    p_down = remote(part.at[0], partr.at[1], psend.at[1], precv.at[1], beside["xm"])
    ways = [
        ("xp", x_up), ("xm", x_down), ("yp", y_up), ("ym", y_down),
        ("zp", z_up), ("zm", z_down), ("xp", p_up), ("xm", p_down),
    ]

    def start(side, copy):
        @pl.when(has[side])
        def _():
            copy.start()

    def arrived(side, copy, buffer, slot):
        @pl.when(has[side])
        def _():
            copy.wait_recv()

        @pl.when(jnp.logical_not(has[side]))
        def _():
            buffer[slot] = jnp.zeros(buffer.shape[1:], buffer.dtype)

    G = jnp.zeros((4 * KL, 128), F)
    lower_y, upper_y = range(0, half, 2), range(half, CY, 2)
    fetch[3, 0].wait()
    stage(3, None, G, lower_y)
    pl.semaphore_wait(barrier, peers)
    start("xp", x_up)
    fetch[0, 1].wait()
    stage(0, None, G, upper_y)
    start("xm", x_down)
    fetch[3, 1].wait()
    stage(3, None, G, upper_y)
    fetch[0, 0].wait()
    stage(0, None, G, lower_y)
    fetch[2, None].wait()
    fetch_s.wait()
    fetch_c.wait()
    G = stage(2, 3, G)
    fetch[1, None].wait()
    for x in range(CX):
        low = m[x, :, 0:16, :].astype(F)[:, 0, :]
        high = m[x, :, CZ - 16 : CZ, :].astype(F)[:, 15, :]
        ok = live_lanes[:CY]
        zs[0, CY * x : CY * (x + 1)] = jnp.where(ok, low, 0.0).astype(BF)
        zs[1, CY * x : CY * (x + 1)] = jnp.where(ok, high, 0.0).astype(BF)
    start("zp", z_up)
    start("zm", z_down)
    G = stage(1, 2, G)
    start("yp", y_up)
    start("ym", y_down)
    G = stage(None, 1, G)
    G = stage(None, 0, G)
    G = G[: 2 * KL] + G[2 * KL :]

    def both(g):
        return jnp.where(live_lanes[:KL, :KS], g[:KL, :KS] + g[KL : 2 * KL, KS:], 0.0)

    def flip(b):
        wide = jnp.concatenate([b, jnp.zeros((KL, KS), F)], 1)
        wide = jnp.concatenate([wide, jnp.zeros((128 - KL, 128), F)], 0)
        return jnp.transpose(wide)[:KL, :KS]

    C = both(G)
    C = 0.5 * (C + flip(C))
    r48 = lax.broadcasted_iota(jnp.int32, (KL, KS), 0)
    l48 = lax.broadcasted_iota(jnp.int32, (KL, KS), 1)
    C = jnp.where((r48 == l48) & (r48 >= count), 1.0, C)

    def both_z(g):
        return -(g[:KL, :KS] + g[KS : KS + KL, KS:])

    arrived("zm", z_up, zr, 0)
    arrived("zp", z_down, zr, 1)
    zp = both_z(lax.dot_general(zs[1], zr[1], TN, preferred_element_type=F))

    mine = lead.at[jnp.minimum(gz, PSUB - 1)]
    mine_sem = lrecv.at[jnp.minimum(gz, PSUB - 1)]
    along = [
        (t, remote(mine, mine, lsend.at[t], mine_sem, {"gx": 0, "gy": 0, "gz": t})) for t in range(PSUB + 1)
    ]
    for k, (ox, oy) in enumerate([(0, 1), (1, 0)]):
        along += [
            (None, remote(mine, mine, lsend.at[(k + 1) * PSUB + 1 + t], mine_sem, {"gx": ox, "gy": oy, "gz": t}))
            for t in range(PSUB)
        ]

    @pl.when(leader)
    def _():
        lead[jnp.minimum(gz, PSUB - 1)] = jnp.concatenate([C, zp], 1)
        for t, copy in along:
            if t is None:
                copy.start()
            else:
                pl.when(gz != t)(copy.start)

    zmT = both_z(lax.dot_general(zr[0], zs[0], TN, preferred_element_type=F))
    zpT = both_z(lax.dot_general(zr[1], zs[1], TN, preferred_element_type=F))

    def face(tiles, own):
        left = jnp.concatenate(tiles, 1)
        right = jnp.concatenate(own, 0)
        return -both(jnp.dot(left, right, preferred_element_type=F))

    arrived("ym", y_up, yr, 0)
    arrived("yp", y_down, yr, 1)
    ymT = face([yr[0, x] for x in range(CX)], [m[x, 0] for x in range(CX)])
    ypT = face([yr[1, x] for x in range(CX)], [m[x, CY - 1] for x in range(CX)])

    def pack(k, a, b):
        gath[gz, k] = jnp.where(core == 1, jnp.concatenate([b, a], 1), jnp.concatenate([a, b], 1))

    zero = jnp.zeros((KL, KS), F)
    pack(0, C, ymT)
    pack(1, ypT, zpT)

    class Gather:
        def __init__(self, at, send, recv, steps):
            give = lambda c, t, k: remote(at(c), at(c), send.at[k], recv.at[c], {"gz": t})
            number = iter(range(15))
            self.steps = [(waits, [give(c, t, next(number)) for c, t in pairs]) for waits, pairs in steps]
            self.sends = [s for _, sends in self.steps for s in sends]
            self.wait = lambda c: remote(at(c), at(c), send.at[0], recv.at[c], {"gz": partner}).wait_recv()

        def step(self, k):
            waits, sends = self.steps[k]
            if len(waits) == len(sends):
                for c, s in zip(waits, sends):
                    self.wait(c)
                    s.start()
                return
            for c in waits:
                self.wait(c)
            for s in sends:
                s.start()

    mine_all = (gz, partner) + around + tuple(also(t) for t in around)
    of_sibling = [t + 1 - 2 * core for t in mine_all]
    far = [also(t) for t in around]
    early = Gather(
        lambda c: gath.at[c, pl.ds(0, 2)], esend, erecv,
        [
            ([], [(gz, t) for t in (partner,) + around + (sibling,)]),
            ([partner], [(partner, t) for t in around + (sibling,)]),
            (list(around), [(t, sibling) for t in around]),
            (far, [(t, sibling) for t in far]),
            (of_sibling, []),
        ],
    )
    late = Gather(
        lambda c: gath.at[c, 2], rsend, rrecv,
        [
            ([], [(gz, t) for t in (partner,) + around + tuple(far) + (sibling,)]),
            ([partner] + list(around) + far, [(t, sibling) for t in [partner] + list(around) + far]),
            (of_sibling, []),
        ],
    )
    early.step(0)

    eye = jnp.where(r48 == l48, 1.0, 0.0)
    for i in range(PSUB):
        b = jnp.where(line0 & (gz == i), C, zero)
        b = jnp.where(line0 & (gz == i - 1), zpT, b)
        b = jnp.where(line0 & (gz == i + 1), zmT, b)
        b = jnp.where((line_y | line_x) & (gz == i), eye, b)
        rhs[i] = b
        xs[i] = zero
    sub[...] = jnp.zeros((KL, 128), F)

    r16 = lax.broadcasted_iota(jnp.int32, (KS - KL, NGZ * KS), 0) + KL
    l16 = lax.rem(lax.broadcasted_iota(jnp.int32, (KS - KL, NGZ * KS), 1), KS)
    out[KL:KS, :] = jnp.where(r16 == l16, 1.0, 0.0)
    for b in range(1, 7):
        out[KS * b + KL : KS * (b + 1), :] = jnp.zeros((KS - KL, NGZ * KS), F)

    def step(i, _):
        @pl.when(jnp.logical_not(line0 & (gz == i)))
        def _():
            remote(lead.at[i], lead.at[i], lsend.at[0], lrecv.at[i], {"gz": partner}).wait_recv()

        g = sub[...]
        a1 = lead[i] - jnp.concatenate([g[:, :KS], zero], 1)
        a2 = jnp.concatenate([rhs[i] - g[:, KS:], zero], 1)
        A = eliminate([[a1[8 * k : 8 * k + 8], a2[8 * k : 8 * k + 8]] for k in range(KL // 8)])
        a1 = jnp.concatenate([a[0] for a in A], 0)
        a2 = jnp.concatenate([a[1] for a in A], 0)
        xs[i] = a2[:, :KS]
        sub[...] = outer_gram(jnp.concatenate([a1[:, KS:], a2[:, :KS]], 1))[:KL]
        return 0

    def chain(low, high):
        @pl.when(chained)
        def _():
            lax.fori_loop(low, high, step, 0)

    chain(0, 1)
    early.step(1)
    chain(1, 3)
    early.step(2)
    arrived("xm", x_up, xr, 0)
    arrived("xp", x_down, xr, 1)
    low = face([xr[0, y] for y in range(half)], [m[0, y] for y in range(half)])
    high = face([xr[1, y] for y in range(half)], [m[CX - 1, half + y] for y in range(half)])
    part[0] = jnp.concatenate([flip(low), zero], 1)
    part[1] = jnp.concatenate([flip(high), zero], 1)
    start("xp", p_up)
    start("xm", p_down)
    early.step(3)
    chain(3, 6)
    arrived("xm", p_up, partr, 0)
    arrived("xp", p_down, partr, 1)
    xmT = low + partr[0, :, :KS]
    pack(2, xmT, high + partr[1, :, :KS])
    late.step(0)
    chain(6, PSUB)

    left = lax.broadcasted_iota(jnp.int32, (KL, 128), 1) < KS

    def lay(p, k, a, b):
        first, second = gath[2 * p, k], gath[2 * p + 1, k]
        cols = slice(128 * p, 128 * (p + 1))
        out[KS * a : KS * a + KL, cols] = jnp.where(left, first, second)
        out[KS * b : KS * b + KL, cols] = pltpu.roll(jnp.where(left, second, first), KS, 1)

    early.step(4)
    for p in range(NGZ // 2):
        lay(p, 0, 0, 3)
        lay(p, 1, 4, 6)
        below = gath[2 * p - 1, 1] if p > 0 else jnp.zeros((KL, 128), F)
        both_below = jnp.where(left, below, gath[2 * p, 1])
        turned = jnp.transpose(jnp.concatenate([both_below, jnp.zeros((128 - KL, 128), F)], 0))
        out[KS * 5 : KS * 5 + KL, 128 * p : 128 * (p + 1)] = jnp.concatenate(
            [turned[:KL, :KS], turned[KS : KS + KL, :KS]], 1
        )

    r64 = lax.broadcasted_iota(jnp.int32, (KS, KS), 0)
    l64 = lax.broadcasted_iota(jnp.int32, (KS, KS), 1)
    dead = jnp.where((r64 == l64) & (r64 >= KL), 1.0, 0.0)
    panel_ref[...] = jnp.zeros((KS, PSUB * KS), F)

    @pl.when(chained)
    def _():
        own = jnp.concatenate([jnp.where(line_y, ymT, xmT), jnp.zeros((KS - KL, KS), F)], 0)
        gap = jnp.zeros((KS - KL, KS), F)
        for p in range(PSUB // 2):
            tops = jnp.concatenate([xs[2 * p], gap, xs[2 * p + 1], gap], 0)
            times = jnp.dot(tops, own, precision=lax.Precision.HIGHEST, preferred_element_type=F)
            tops = jnp.where(line0, tops, times)
            tops = jnp.concatenate([tops, jnp.zeros((128, KS), F)], 1)
            ends = jnp.concatenate(
                [jnp.where(line0 & (gz == 2 * p + k), dead, jnp.zeros((KS, KS), F)) for k in range(2)], 1
            )
            panel_ref[:, 128 * p : 128 * (p + 1)] = jnp.transpose(tops)[:KS] + ends

    late.step(1)
    late.step(2)
    for p in range(NGZ // 2):
        lay(p, 2, 1, 2)

    for s in early.sends + late.sends:
        s.wait_send()
    for side, copy in ways:
        @pl.when(has[side])
        def _():
            copy.wait_send()

    @pl.when(leader)
    def _():
        for t, copy in along:
            if t is None:
                copy.wait_send()
            else:
                pl.when(gz != t)(copy.wait_send)


def local(vectors, diag_shift, coupling, counts):
    dma = pltpu.SemaphoreType.DMA
    columns, panel = pl.pallas_call(
        kernel,
        out_shape=(
            jax.ShapeDtypeStruct((7 * KS, NGZ * KS), F),
            jax.ShapeDtypeStruct((KS, PSUB * KS), F),
        ),
        in_specs=[pl.BlockSpec(memory_space=pltpu.SMEM)] + [pl.BlockSpec(memory_space=pltpu.HBM)] * 3,
        out_specs=(pl.BlockSpec(memory_space=pltpu.VMEM), pl.BlockSpec(memory_space=pltpu.VMEM)),
        scratch_shapes=[
            pltpu.VMEM((CX, CY, CZ, 128), BF),
            pltpu.VMEM((CX, CY, 2 * KL, CZ), BF),
            pltpu.VMEM((2, CX, CY, CZ), F),
            pltpu.VMEM((CX, CY, CZ), F),
            pltpu.VMEM((2, CY // 2, 2 * KL, CZ), BF),
            pltpu.VMEM((2, CX, 2 * KL, CZ), BF),
            pltpu.VMEM((2, CX * CY, 128), BF),
            pltpu.VMEM((2, CX * CY, 128), BF),
            pltpu.VMEM((2, KL, 128), F),
            pltpu.VMEM((2, KL, 128), F),
            pltpu.VMEM((PSUB, KL, 128), F),
            pltpu.VMEM((PSUB, KL, KS), F),
            pltpu.VMEM((PSUB, KL, KS), F),
            pltpu.VMEM((KL, 128), F),
            pltpu.VMEM((NGZ, 3, KL, 128), F),
            dma((8,)),
            dma((2,)), dma((2,)), dma((2,)), dma((2,)), dma((2,)), dma((2,)), dma((2,)), dma((2,)),
            dma((3 * PSUB + 1,)), dma((PSUB,)), dma((15,)), dma((NGZ,)), dma((15,)), dma((NGZ,)),
        ],
        compiler_params=pltpu.CompilerParams(
            collective_id=0, has_side_effects=True, vmem_limit_bytes=(50 << 20) + (100 << 10)
        ),
    )(counts, vectors, diag_shift, coupling)
    return columns.T, panel


def solution(mesh):
    return jax.shard_map(
        local,
        mesh=mesh,
        in_specs=(
            P("gx", "gy", "gz", None),
            P(None, "gx", "gy", "gz"),
            P("gx", "gy", "gz"),
            P(("gx", "gy", "gz")),
        ),
        out_specs=(P(("gx", "gy"), None), P(("gx", "gy", "gz"), None)),
        check_vma=False,
    )
```

```python
import jax
import jax.numpy as jnp
from jax import lax
from jax.experimental import pallas as pl
from jax.experimental.pallas import tpu as pltpu
from jax.sharding import PartitionSpec as P

F = jnp.float32
BF = jnp.bfloat16
CX, CY, CZ = 4, 16, 128
KS = 64
KL = 48
PSUB = 8
NGX, NGY, NGZ = 4, 4, 16
GROUP = 16
MESH = pl.DeviceIdType.MESH


def remote(src, dst, send, recv, device):
    return pltpu.make_async_remote_copy(
        src_ref=src, dst_ref=dst, send_sem=send, recv_sem=recv, device_id=device, device_id_type=MESH
    )


def lanes_of(x, c):
    return jnp.broadcast_to(x[:, c : c + 1], (8, 128))


def rows_of(x, r):
    return jnp.broadcast_to(x[r : r + 1, :], (8, 128))


def eliminate(A):
    rows = lax.broadcasted_iota(jnp.int32, (8, 128), 0)
    n = KL // 8
    for first in range(0, KL, GROUP):
        copies = [[None] * n for _ in range(GROUP)]
        for c in range(GROUP):
            for i in range(first // 8, n):
                copies[c][i] = lanes_of(A[i][0], first + c)
        p = rows_of(copies[0][first // 8], 0)
        for c in range(GROUP):
            J, s = (first + c) // 8, c % 8
            if c + 1 < GROUP:
                ahead = rows_of(copies[c + 1][(first + c + 1) // 8], (c + 1) % 8)
            r = lax.rsqrt(p)
            row = [rows_of(a, s) * r for a in A[J]]
            beside = [rows_of(copies[k][J], s) * r for k in range(c + 1, GROUP)]
            if c + 1 < GROUP:
                p = ahead - beside[0] * beside[0]
            for i in range(J, n):
                f = copies[c][i] * r
                if i == J:
                    f = jnp.where(rows > s, f, 0.0)
                for q in range(len(row)):
                    A[i][q] = A[i][q] - f * row[q]
                for k in range(c + 1, GROUP):
                    copies[k][i] = copies[k][i] - f * beside[k - c - 1]
            for q in range(len(row)):
                A[J][q] = jnp.where(rows == s, row[q], A[J][q])
    return A


def split3(x):
    h = x.astype(BF)
    x = x - h.astype(F)
    m = x.astype(BF)
    x = x - m.astype(F)
    return h, m, x.astype(BF)


TN = (((0,), (0,)), ((), ()))


def outer_gram(W, X):
    wh, wm, wl = split3(W)
    h, m, low = split3(X)
    left1, right1 = jnp.concatenate([wh, wh, wm], 0), jnp.concatenate([h, m, h], 0)
    left2, right2 = jnp.concatenate([wm, wh, wl], 0), jnp.concatenate([m, low, h], 0)
    return lax.dot_general(left1, right1, TN, preferred_element_type=F) + lax.dot_general(
        left2, right2, TN, preferred_element_type=F
    )


def kernel(
    cnt_ref, m_hbm, s_hbm, out, panel_ref,
    m, tt, sh, xr, yr, zs, zr, part, partr, lead, rhs, xs, sub, gath, post, postr,
    ready, load, xsend, xrecv, ysend, yrecv, zsend, zrecv, psend, precv, lsend, lrecv, osend, orecv, esend, erecv, rsend, rrecv,
):
    gx, gy, gz = lax.axis_index("gx"), lax.axis_index("gy"), lax.axis_index("gz")
    has = {
        "xm": gx > 0, "xp": gx < NGX - 1,
        "ym": gy > 0, "yp": gy < NGY - 1,
        "zm": gz > 0, "zp": gz < NGZ - 1,
    }
    beside = {
        "xm": {"gx": gx - 1}, "xp": {"gx": gx + 1},
        "ym": {"gy": gy - 1}, "yp": {"gy": gy + 1},
        "zm": {"gz": gz - 1}, "zp": {"gz": gz + 1},
    }
    barrier = pltpu.get_barrier_semaphore()
    core = lax.rem(gz, 2)
    partner = lax.rem(gz + 8, NGZ)
    sibling = gz + 1 - 2 * core
    plane = 8 * (gz // 8)
    ring = lambda k: plane + lax.rem(gz - plane + 2 * k, 8)
    up, opposite, down = ring(1), ring(2), ring(3)
    line0 = (gx == 0) & (gy == 0)
    line_y = (gx == 0) & (gy == 1)
    line_x = (gx == 1) & (gy == 0)
    leader = line0 & (gz < PSUB)
    chained = line0 & (gz <= PSUB)
    follower = (line_y | line_x) & (gz < PSUB)

    also = lambda c: lax.rem(c + 8, NGZ)
    around = (up, down, opposite)
    for t in (partner, sibling) + around + tuple(also(t) for t in around):
        pl.semaphore_signal(barrier, inc=1, device_id={"gz": t}, device_id_type=MESH)
    peers = 8
    for side, other in (("xp", "xm"), ("ym", "ym"), ("yp", "yp"), ("zm", "zm"), ("zp", "zp")):
        @pl.when(has[side])
        def _():
            pl.semaphore_signal(barrier, inc=1, device_id=beside[side], device_id_type=MESH)

        peers = peers + has[other].astype(jnp.int32)
    for t in range(PSUB):
        @pl.when(chained & (gz != t))
        def _():
            pl.semaphore_signal(barrier, inc=1, device_id={"gz": t}, device_id_type=MESH)
    peers = peers + jnp.where(leader, PSUB, 0)

    half = CY // 2
    fetch = {}
    for k, (x, h) in enumerate([(3, 0), (0, 1), (3, 1), (0, 0), (2, None), (1, None)]):
        part_of = (x,) if h is None else (x, pl.ds(half * h, half))
        fetch[x, h] = pltpu.make_async_copy(m_hbm.at[part_of], m.at[part_of], load.at[k])
        fetch[x, h].start()
    fetch_s = pltpu.make_async_copy(s_hbm, sh, load.at[6])
    fetch_s.start()

    count = cnt_ref[0]
    r128 = lax.broadcasted_iota(jnp.int32, (128, 128), 0)
    l128 = lax.broadcasted_iota(jnp.int32, (128, 128), 1)
    live_rows = (jnp.where(r128 >= KS, r128 - KS, r128) < count).astype(F).astype(BF)
    live_lanes = (jnp.where(l128 >= KS, l128 - KS, l128) < count)[:KS]

    inner_z = jnp.where(lax.broadcasted_iota(jnp.int32, (KL, 128), 1) < CZ - 1, 1.0, 0.0)

    def transpose(x, y):
        t = jnp.swapaxes(m[x, y], 0, 1) * live_rows
        tt[x, y, 0:KL] = t[0:KL]
        tt[x, y, KL : 2 * KL] = t[KS : KS + KL]

    def image(x, y):
        wide = (KL, 128)
        a0 = jnp.broadcast_to(sh[0, x, y : y + 1, :] + 6.0, wide)
        a1 = jnp.broadcast_to(sh[1, x, y : y + 1, :] + 6.0, wide)
        c = jnp.broadcast_to(sh[2, x, y : y + 1, :], wide)
        u = tt[x, y, 0:KL, :].astype(F)
        v = tt[x, y, KL : 2 * KL, :].astype(F)

        def forward(w, at):
            n = pltpu.roll(w, CZ - 1, 1) * inner_z
            if y < CY - 1:
                n = n + tt[x, y + 1, at : at + KL, :].astype(F)
            if x < CX - 1:
                n = n + tt[x + 1, y, at : at + KL, :].astype(F)
            return n

        yu = a0 * u + c * v - 2.0 * forward(u, 0)
        yv = a1 * v + c * u - 2.0 * forward(v, KL)
        high = [w.astype(BF) for w in (yu, yv)]
        return jnp.concatenate(high + [(w - h.astype(F)).astype(BF) for w, h in zip((yu, yv), high)], 0)

    def stage(tx, yx, G, ys=range(0, CY, 2)):
        for y in ys:
            if tx is not None:
                transpose(tx, y)
                transpose(tx, y + 1)
            if yx is not None:
                left = jnp.concatenate([image(yx, y), image(yx, y + 1)], 1)
                right = jnp.concatenate([m[yx, y], m[yx, y + 1]], 0)
                G = G + jnp.dot(left, right, preferred_element_type=F)
        return G

    x_up = remote(tt.at[3, pl.ds(0, half)], xr.at[0], xsend.at[0], xrecv.at[0], beside["xp"])
    x_down = remote(tt.at[0, pl.ds(half, half)], xr.at[1], xsend.at[1], xrecv.at[1], beside["xm"])
    y_up = remote(tt.at[:, CY - 1], yr.at[0], ysend.at[0], yrecv.at[0], beside["yp"])
    y_down = remote(tt.at[:, 0], yr.at[1], ysend.at[1], yrecv.at[1], beside["ym"])
    z_up = remote(zs.at[1], zr.at[0], zsend.at[0], zrecv.at[0], beside["zp"])
    z_down = remote(zs.at[0], zr.at[1], zsend.at[1], zrecv.at[1], beside["zm"])
    p_up = remote(part.at[1], partr.at[0], psend.at[0], precv.at[0], beside["xp"])
    p_down = remote(part.at[0], partr.at[1], psend.at[1], precv.at[1], beside["xm"])
    ways = [
        ("xp", x_up), ("xm", x_down), ("yp", y_up), ("ym", y_down),
        ("zp", z_up), ("zm", z_down), ("xp", p_up), ("xm", p_down),
    ]

    def start(side, copy):
        @pl.when(has[side])
        def _():
            copy.start()

    def arrived(side, copy, buffer, slot):
        @pl.when(has[side])
        def _():
            copy.wait_recv()

        @pl.when(jnp.logical_not(has[side]))
        def _():
            buffer[slot] = jnp.zeros(buffer.shape[1:], buffer.dtype)

    G = jnp.zeros((4 * KL, 128), F)
    lower_y, upper_y = range(0, half, 2), range(half, CY, 2)
    fetch[3, 0].wait()
    stage(3, None, G, lower_y)

    @pl.when(has["xm"])
    def _():
        pl.semaphore_wait(barrier, peers)
        pl.semaphore_signal(ready, inc=1, device_id=beside["xm"], device_id_type=MESH)

    fetch[0, 1].wait()
    stage(0, None, G, upper_y)
    start("xm", x_down)

    @pl.when(has["xm"] & has["xp"])
    def _():
        pl.semaphore_wait(ready, 1)
        x_up.start()

    fetch[3, 1].wait()
    stage(3, None, G, upper_y)
    fetch[0, 0].wait()
    stage(0, None, G, lower_y)
    fetch[2, None].wait()
    fetch_s.wait()
    G = stage(2, 3, G)

    @pl.when(jnp.logical_not(has["xm"]))
    def _():
        pl.semaphore_wait(barrier, peers)

    fetch[1, None].wait()
    for x in range(CX):
        low = m[x, :, 0:16, :].astype(F)[:, 0, :]
        high = m[x, :, CZ - 16 : CZ, :].astype(F)[:, 15, :]
        ok = live_lanes[:CY]
        zs[0, CY * x : CY * (x + 1)] = jnp.where(ok, low, 0.0).astype(BF)
        zs[1, CY * x : CY * (x + 1)] = jnp.where(ok, high, 0.0).astype(BF)
    start("zp", z_up)
    start("zm", z_down)
    G = stage(1, 2, G)
    start("yp", y_up)
    start("ym", y_down)
    G = stage(None, 1, G)
    G = stage(None, 0, G)
    G = G[: 2 * KL] + G[2 * KL :]

    def both(g):
        return jnp.where(live_lanes[:KL, :KS], g[:KL, :KS] + g[KL : 2 * KL, KS:], 0.0)

    def flip(b):
        wide = jnp.concatenate([b, jnp.zeros((KL, KS), F)], 1)
        wide = jnp.concatenate([wide, jnp.zeros((128 - KL, 128), F)], 0)
        return jnp.transpose(wide)[:KL, :KS]

    C = both(G)
    C = 0.5 * (C + flip(C))
    r48 = lax.broadcasted_iota(jnp.int32, (KL, KS), 0)
    l48 = lax.broadcasted_iota(jnp.int32, (KL, KS), 1)
    C = jnp.where((r48 == l48) & (r48 >= count), 1.0, C)

    def both_z(g):
        return -(g[:KL, :KS] + g[KS : KS + KL, KS:])

    arrived("zm", z_up, zr, 0)
    arrived("zp", z_down, zr, 1)
    zp = both_z(lax.dot_general(zs[1], zr[1], TN, preferred_element_type=F))

    mine = lead.at[jnp.minimum(gz, PSUB - 1)]
    mine_sem = lrecv.at[jnp.minimum(gz, PSUB - 1)]
    along = [remote(mine, mine, lsend.at[t], mine_sem, {"gz": t}) for t in range(PSUB + 1)]

    @pl.when(leader)
    def _():
        lead[jnp.minimum(gz, PSUB - 1)] = jnp.concatenate([C, zp], 1)
        for t in range(PSUB + 1):
            pl.when(gz != t)(along[t].start)

    @pl.when(jnp.logical_not(has["xm"]))
    def _():
        pl.semaphore_wait(ready, 1)
        x_up.start()

    zmT = both_z(lax.dot_general(zr[0], zs[0], TN, preferred_element_type=F))
    zpT = both_z(lax.dot_general(zr[1], zs[1], TN, preferred_element_type=F))

    def face(tiles, own):
        left = jnp.concatenate(tiles, 1)
        right = jnp.concatenate(own, 0)
        return -both(jnp.dot(left, right, preferred_element_type=F))

    arrived("ym", y_up, yr, 0)
    arrived("yp", y_down, yr, 1)
    ymT = face([yr[0, x] for x in range(CX)], [m[x, 0] for x in range(CX)])
    ypT = face([yr[1, x] for x in range(CX)], [m[x, CY - 1] for x in range(CX)])

    def pack(k, a, b):
        gath[gz, k] = jnp.where(core == 1, jnp.concatenate([b, a], 1), jnp.concatenate([a, b], 1))

    zero = jnp.zeros((KL, KS), F)
    pack(0, C, ymT)
    pack(1, ypT, zpT)

    class Gather:
        def __init__(self, at, send, recv, steps):
            give = lambda c, t, k: remote(at(c), at(c), send.at[k], recv.at[c], {"gz": t})
            number = iter(range(15))
            self.steps = [(waits, [give(c, t, next(number)) for c, t in pairs]) for waits, pairs in steps]
            self.sends = [s for _, sends in self.steps for s in sends]
            self.wait = lambda c: remote(at(c), at(c), send.at[0], recv.at[c], {"gz": partner}).wait_recv()

        def step(self, k):
            waits, sends = self.steps[k]
            if len(waits) == len(sends):
                for c, s in zip(waits, sends):
                    self.wait(c)
                    s.start()
                return
            for c in waits:
                self.wait(c)
            for s in sends:
                s.start()

    mine_all = (gz, partner) + around + tuple(also(t) for t in around)
    of_sibling = [t + 1 - 2 * core for t in mine_all]
    far = [also(t) for t in around]
    early = Gather(
        lambda c: gath.at[c, pl.ds(0, 2)], esend, erecv,
        [
            ([], [(gz, t) for t in (partner,) + around + (sibling,)]),
            ([partner], [(partner, t) for t in around + (sibling,)]),
            (list(around), [(t, sibling) for t in around]),
            (far, [(t, sibling) for t in far]),
            (of_sibling, []),
        ],
    )
    late = Gather(
        lambda c: gath.at[c, 2], rsend, rrecv,
        [
            ([], [(gz, t) for t in (partner,) + around + tuple(far) + (sibling,)]),
            ([partner] + list(around) + far, [(t, sibling) for t in [partner] + list(around) + far]),
            (of_sibling, []),
        ],
    )
    early.step(0)

    eye = jnp.where(r48 == l48, 1.0, 0.0)
    for i in range(PSUB):
        b = jnp.where(gz == i, C, zero)
        b = jnp.where(gz == i - 1, zpT, b)
        b = jnp.where(gz == i + 1, zmT, b)
        rhs[i] = jnp.concatenate([b, jnp.where(gz == i, eye, zero)], 1)
        xs[i] = jnp.zeros((KL, 128), F)
    sub[...] = jnp.zeros((KL, 256), F)

    r16 = lax.broadcasted_iota(jnp.int32, (KS - KL, NGZ * KS), 0) + KL
    l16 = lax.rem(lax.broadcasted_iota(jnp.int32, (KS - KL, NGZ * KS), 1), KS)
    out[KL:KS, :] = jnp.where(r16 == l16, 1.0, 0.0)
    for b in range(1, 7):
        out[KS * b + KL : KS * (b + 1), :] = jnp.zeros((KS - KL, NGZ * KS), F)

    first_lanes = lax.broadcasted_iota(jnp.int32, (KL, 128), 1) < KS

    def step(i, _):
        @pl.when(gz != i)
        def _():
            remote(lead.at[i], lead.at[i], lsend.at[0], lrecv.at[i], {"gz": partner}).wait_recv()

        g = sub[...]
        a1 = lead[i] - jnp.where(first_lanes, g[:, :128], 0.0)
        a2 = rhs[i] - g[:, 128:]
        A = eliminate([[a1[8 * k : 8 * k + 8], a2[8 * k : 8 * k + 8]] for k in range(KL // 8)])
        a1 = jnp.concatenate([a[0] for a in A], 0)
        a2 = jnp.concatenate([a[1] for a in A], 0)
        xs[i] = a2
        turned = pltpu.roll(a1, KS, 1)
        sub[...] = outer_gram(turned[:, :KS], jnp.concatenate([turned, a2], 1))[:KL]
        return 0

    def chain(low, high):
        @pl.when(chained)
        def _():
            lax.fori_loop(low, high, step, 0)

    early.step(1)
    chain(0, 2)
    early.step(2)
    arrived("xm", x_up, xr, 0)
    low = face([xr[0, y] for y in range(half)], [m[0, y] for y in range(half)])
    part[0] = jnp.concatenate([flip(low), zero], 1)
    start("xm", p_down)
    arrived("xp", x_down, xr, 1)
    high = face([xr[1, y] for y in range(half)], [m[CX - 1, half + y] for y in range(half)])
    part[1] = jnp.concatenate([flip(high), zero], 1)
    start("xp", p_up)
    chain(2, 5)
    arrived("xm", p_up, partr, 0)
    arrived("xp", p_down, partr, 1)
    xpT = high + partr[1, :, :KS]
    pack(2, low + partr[0, :, :KS], xpT)
    late.step(0)
    early.step(3)
    chain(5, PSUB)

    to_y = remote(post.at[0], postr, osend.at[0], orecv, beside["yp"])
    to_x = remote(post.at[1], postr, osend.at[1], orecv, beside["xp"])

    @pl.when(leader)
    def _():
        right = jnp.concatenate([flip(ypT), flip(xpT)], 1)
        wide = [
            jnp.dot(xs[i][:, KS : KS + KL], right, precision=lax.Precision.HIGHEST, preferred_element_type=F)
            for i in range(PSUB)
        ]
        for p in range(PSUB // 2):
            a, b = wide[2 * p], wide[2 * p + 1]
            post[0, p] = jnp.concatenate([a[:, :KS], b[:, :KS]], 1)
            post[1, p] = jnp.concatenate([a[:, KS:], b[:, KS:]], 1)
        to_y.start()
        to_x.start()


    left = lax.broadcasted_iota(jnp.int32, (KL, 128), 1) < KS

    def lay(p, k, a, b):
        first, second = gath[2 * p, k], gath[2 * p + 1, k]
        cols = slice(128 * p, 128 * (p + 1))
        out[KS * a : KS * a + KL, cols] = jnp.where(left, first, second)
        out[KS * b : KS * b + KL, cols] = pltpu.roll(jnp.where(left, second, first), KS, 1)

    early.step(4)
    for p in range(NGZ // 2):
        lay(p, 0, 0, 3)
        lay(p, 1, 4, 6)
        below = gath[2 * p - 1, 1] if p > 0 else jnp.zeros((KL, 128), F)
        both_below = jnp.where(left, below, gath[2 * p, 1])
        turned = jnp.transpose(jnp.concatenate([both_below, jnp.zeros((128 - KL, 128), F)], 0))
        out[KS * 5 : KS * 5 + KL, 128 * p : 128 * (p + 1)] = jnp.concatenate(
            [turned[:KL, :KS], turned[KS : KS + KL, :KS]], 1
        )

    def put_panel(p, tile, ends):
        t = jnp.transpose(jnp.concatenate([tile, jnp.zeros((128 - KL, 128), F)], 0))
        panel_ref[:, 128 * p : 128 * (p + 1)] = jnp.concatenate([t[:KS, :KS], t[KS:, :KS]], 1) + ends

    panel_ref[...] = jnp.zeros((KS, PSUB * KS), F)

    @pl.when(chained)
    def _():
        r64 = lax.broadcasted_iota(jnp.int32, (KS, KS), 0)
        l64 = lax.broadcasted_iota(jnp.int32, (KS, KS), 1)
        dead = jnp.where((r64 == l64) & (r64 >= KL), 1.0, 0.0)
        for p in range(PSUB // 2):
            ends = [jnp.where(gz == 2 * p + k, dead, jnp.zeros((KS, KS), F)) for k in range(2)]
            tile = jnp.concatenate([xs[2 * p][:, :KS], xs[2 * p + 1][:, :KS]], 1)
            put_panel(p, tile, jnp.concatenate(ends, 1))

    late.step(1)
    late.step(2)
    for p in range(NGZ // 2):
        lay(p, 2, 1, 2)

    @pl.when(follower)
    def _():
        to_y.wait_recv()
        for p in range(PSUB // 2):
            put_panel(p, postr[p], 0.0)

    for s in early.sends + late.sends:
        s.wait_send()
    for side, copy in ways:
        @pl.when(has[side])
        def _():
            copy.wait_send()

    @pl.when(leader)
    def _():
        to_y.wait_send()
        to_x.wait_send()
        for t in range(PSUB + 1):
            pl.when(gz != t)(along[t].wait_send)


def local(vectors, diag_shift, coupling, counts):
    dma = pltpu.SemaphoreType.DMA
    columns, panel = pl.pallas_call(
        kernel,
        out_shape=(
            jax.ShapeDtypeStruct((7 * KS, NGZ * KS), F),
            jax.ShapeDtypeStruct((KS, PSUB * KS), F),
        ),
        in_specs=[pl.BlockSpec(memory_space=pltpu.SMEM)] + [pl.BlockSpec(memory_space=pltpu.HBM)] * 2,
        out_specs=(pl.BlockSpec(memory_space=pltpu.VMEM), pl.BlockSpec(memory_space=pltpu.VMEM)),
        scratch_shapes=[
            pltpu.VMEM((CX, CY, CZ, 128), BF),
            pltpu.VMEM((CX, CY, 2 * KL, CZ), BF),
            pltpu.VMEM((3, CX, CY, CZ), F),
            pltpu.VMEM((2, CY // 2, 2 * KL, CZ), BF),
            pltpu.VMEM((2, CX, 2 * KL, CZ), BF),
            pltpu.VMEM((2, CX * CY, 128), BF),
            pltpu.VMEM((2, CX * CY, 128), BF),
            pltpu.VMEM((2, KL, 128), F),
            pltpu.VMEM((2, KL, 128), F),
            pltpu.VMEM((PSUB, KL, 128), F),
            pltpu.VMEM((PSUB, KL, 128), F),
            pltpu.VMEM((PSUB, KL, 128), F),
            pltpu.VMEM((KL, 256), F),
            pltpu.VMEM((NGZ, 3, KL, 128), F),
            pltpu.VMEM((2, PSUB // 2, KL, 128), F),
            pltpu.VMEM((PSUB // 2, KL, 128), F),
            pltpu.SemaphoreType.REGULAR,
            dma((7,)),
            dma((2,)), dma((2,)), dma((2,)), dma((2,)), dma((2,)), dma((2,)), dma((2,)), dma((2,)),
            dma((PSUB + 1,)), dma((PSUB,)), dma((2,)), dma, dma((15,)), dma((NGZ,)), dma((15,)), dma((NGZ,)),
        ],
        compiler_params=pltpu.CompilerParams(
            collective_id=0, has_side_effects=True, vmem_limit_bytes=(50 << 20) + (100 << 10)
        ),
    )(counts, vectors, jnp.concatenate([diag_shift, coupling[None]], 0))
    return columns.T, panel


def solution(mesh):
    return jax.shard_map(
        local,
        mesh=mesh,
        in_specs=(
            P("gx", "gy", "gz", None),
            P(None, "gx", "gy", "gz"),
            P("gx", "gy", "gz"),
            P(("gx", "gy", "gz")),
        ),
        out_specs=(P(("gx", "gy"), None), P(("gx", "gy", "gz"), None)),
        check_vma=False,
    )
```

```python
import jax
import jax.numpy as jnp
from jax import lax
from jax.experimental import pallas as pl
from jax.experimental.pallas import tpu as pltpu
from jax.sharding import PartitionSpec as P

F = jnp.float32
BF = jnp.bfloat16
CX, CY, CZ = 4, 16, 128
KS = 64
KL = 48
PSUB = 8
NGX, NGY, NGZ = 4, 4, 16
GROUP = 16
MESH = pl.DeviceIdType.MESH


def remote(src, dst, send, recv, device):
    return pltpu.make_async_remote_copy(
        src_ref=src, dst_ref=dst, send_sem=send, recv_sem=recv, device_id=device, device_id_type=MESH
    )


def lanes_of(x, c):
    return jnp.broadcast_to(x[:, c : c + 1], (8, 128))


def rows_of(x, r):
    return jnp.broadcast_to(x[r : r + 1, :], (8, 128))


def eliminate(A):
    rows = lax.broadcasted_iota(jnp.int32, (8, 128), 0)
    n = KL // 8
    for first in range(0, KL, GROUP):
        copies = [[None] * n for _ in range(GROUP)]
        for c in range(GROUP):
            for i in range(first // 8, n):
                copies[c][i] = lanes_of(A[i][0], first + c)
        p = rows_of(copies[0][first // 8], 0)
        for c in range(GROUP):
            J, s = (first + c) // 8, c % 8
            if c + 1 < GROUP:
                ahead = rows_of(copies[c + 1][(first + c + 1) // 8], (c + 1) % 8)
            r = lax.rsqrt(p)
            row = [rows_of(a, s) * r for a in A[J]]
            beside = [rows_of(copies[k][J], s) * r for k in range(c + 1, GROUP)]
            if c + 1 < GROUP:
                p = ahead - beside[0] * beside[0]
            for i in range(J, n):
                f = copies[c][i] * r
                if i == J:
                    f = jnp.where(rows > s, f, 0.0)
                for q in range(len(row)):
                    A[i][q] = A[i][q] - f * row[q]
                for k in range(c + 1, GROUP):
                    copies[k][i] = copies[k][i] - f * beside[k - c - 1]
            for q in range(len(row)):
                A[J][q] = jnp.where(rows == s, row[q], A[J][q])
    return A


def split3(x):
    h = x.astype(BF)
    x = x - h.astype(F)
    m = x.astype(BF)
    x = x - m.astype(F)
    return h, m, x.astype(BF)


TN = (((0,), (0,)), ((), ()))


def outer_gram(W, X):
    wh, wm, wl = split3(W)
    h, m, low = split3(X)
    left1, right1 = jnp.concatenate([wh, wh, wm], 0), jnp.concatenate([h, m, h], 0)
    left2, right2 = jnp.concatenate([wm, wh, wl], 0), jnp.concatenate([m, low, h], 0)
    return lax.dot_general(left1, right1, TN, preferred_element_type=F) + lax.dot_general(
        left2, right2, TN, preferred_element_type=F
    )


def kernel(
    cnt_ref, m_hbm, s_hbm, out, panel_ref,
    m, tt, sh, xr, yr, zs, zr, part, partr, lead, rhs, xs, sub, gath, post, postr,
    ready, load, xsend, xrecv, ysend, yrecv, zsend, zrecv, psend, precv, lsend, lrecv, osend, orecv, esend, erecv, rsend, rrecv,
):
    gx, gy, gz = lax.axis_index("gx"), lax.axis_index("gy"), lax.axis_index("gz")
    has = {
        "xm": gx > 0, "xp": gx < NGX - 1,
        "ym": gy > 0, "yp": gy < NGY - 1,
        "zm": gz > 0, "zp": gz < NGZ - 1,
    }
    beside = {
        "xm": {"gx": gx - 1}, "xp": {"gx": gx + 1},
        "ym": {"gy": gy - 1}, "yp": {"gy": gy + 1},
        "zm": {"gz": gz - 1}, "zp": {"gz": gz + 1},
    }
    barrier = pltpu.get_barrier_semaphore()
    core = lax.rem(gz, 2)
    partner = lax.rem(gz + 8, NGZ)
    sibling = gz + 1 - 2 * core
    plane = 8 * (gz // 8)
    ring = lambda k: plane + lax.rem(gz - plane + 2 * k, 8)
    up, opposite, down = ring(1), ring(2), ring(3)
    line0 = (gx == 0) & (gy == 0)
    line_y = (gx == 0) & (gy == 1)
    line_x = (gx == 1) & (gy == 0)
    leader = line0 & (gz < PSUB)
    chained = line0 & (gz <= PSUB)
    follower = (line_y | line_x) & (gz < PSUB)

    also = lambda c: lax.rem(c + 8, NGZ)
    around = (up, down, opposite)
    for t in (partner, sibling) + around + tuple(also(t) for t in around):
        pl.semaphore_signal(barrier, inc=1, device_id={"gz": t}, device_id_type=MESH)
    peers = 8
    for side, other in (("xp", "xm"), ("ym", "ym"), ("yp", "yp"), ("zm", "zm"), ("zp", "zp")):
        @pl.when(has[side])
        def _():
            pl.semaphore_signal(barrier, inc=1, device_id=beside[side], device_id_type=MESH)

        peers = peers + has[other].astype(jnp.int32)
    for t in range(PSUB):
        @pl.when(chained & (gz != t))
        def _():
            pl.semaphore_signal(barrier, inc=1, device_id={"gz": t}, device_id_type=MESH)
    peers = peers + jnp.where(leader, PSUB, 0)

    half = CY // 2
    fetch = {}
    for k, (x, h) in enumerate([(3, 0), (0, 1), (3, 1), (0, 0), (2, None), (1, None)]):
        part_of = (x,) if h is None else (x, pl.ds(half * h, half))
        fetch[x, h] = pltpu.make_async_copy(m_hbm.at[part_of], m.at[part_of], load.at[k])
        fetch[x, h].start()
    fetch_s = pltpu.make_async_copy(s_hbm, sh, load.at[6])
    fetch_s.start()

    count = cnt_ref[0]
    r128 = lax.broadcasted_iota(jnp.int32, (128, 128), 0)
    l128 = lax.broadcasted_iota(jnp.int32, (128, 128), 1)
    live_rows = (jnp.where(r128 >= KS, r128 - KS, r128) < count).astype(F).astype(BF)
    live_lanes = (jnp.where(l128 >= KS, l128 - KS, l128) < count)[:KS]

    inner_z = jnp.where(lax.broadcasted_iota(jnp.int32, (KL, 128), 1) < CZ - 1, 1.0, 0.0)

    def transpose(x, y):
        t = jnp.swapaxes(m[x, y], 0, 1) * live_rows
        tt[x, y, 0:KL] = t[0:KL]
        tt[x, y, KL : 2 * KL] = t[KS : KS + KL]

    def image(x, y):
        wide = (KL, 128)
        a0 = jnp.broadcast_to(sh[0, x, y : y + 1, :] + 6.0, wide)
        a1 = jnp.broadcast_to(sh[1, x, y : y + 1, :] + 6.0, wide)
        c = jnp.broadcast_to(sh[2, x, y : y + 1, :], wide)
        u = tt[x, y, 0:KL, :].astype(F)
        v = tt[x, y, KL : 2 * KL, :].astype(F)

        def forward(w, at):
            n = pltpu.roll(w, CZ - 1, 1) * inner_z
            if y < CY - 1:
                n = n + tt[x, y + 1, at : at + KL, :].astype(F)
            if x < CX - 1:
                n = n + tt[x + 1, y, at : at + KL, :].astype(F)
            return n

        yu = a0 * u + c * v - 2.0 * forward(u, 0)
        yv = a1 * v + c * u - 2.0 * forward(v, KL)
        high = [w.astype(BF) for w in (yu, yv)]
        return jnp.concatenate(high + [(w - h.astype(F)).astype(BF) for w, h in zip((yu, yv), high)], 0)

    def stage(tx, yx, G, ys=range(0, CY, 2)):
        for y in ys:
            if tx is not None:
                transpose(tx, y)
                transpose(tx, y + 1)
            if yx is not None:
                left = jnp.concatenate([image(yx, y), image(yx, y + 1)], 1)
                right = jnp.concatenate([m[yx, y], m[yx, y + 1]], 0)
                G = G + jnp.dot(left, right, preferred_element_type=F)
        return G

    x_up = remote(tt.at[3, pl.ds(0, half)], xr.at[0], xsend.at[0], xrecv.at[0], beside["xp"])
    x_down = remote(tt.at[0, pl.ds(half, half)], xr.at[1], xsend.at[1], xrecv.at[1], beside["xm"])
    y_up = remote(tt.at[:, CY - 1], yr.at[0], ysend.at[0], yrecv.at[0], beside["yp"])
    y_down = remote(tt.at[:, 0], yr.at[1], ysend.at[1], yrecv.at[1], beside["ym"])
    z_up = remote(zs.at[1], zr.at[0], zsend.at[0], zrecv.at[0], beside["zp"])
    z_down = remote(zs.at[0], zr.at[1], zsend.at[1], zrecv.at[1], beside["zm"])
    p_up = remote(part.at[1], partr.at[0], psend.at[0], precv.at[0], beside["xp"])
    p_down = remote(part.at[0], partr.at[1], psend.at[1], precv.at[1], beside["xm"])
    ways = [
        ("xp", x_up), ("xm", x_down), ("yp", y_up), ("ym", y_down),
        ("zp", z_up), ("zm", z_down), ("xp", p_up), ("xm", p_down),
    ]

    def start(side, copy):
        @pl.when(has[side])
        def _():
            copy.start()

    def arrived(side, copy, buffer, slot):
        @pl.when(has[side])
        def _():
            copy.wait_recv()

        @pl.when(jnp.logical_not(has[side]))
        def _():
            buffer[slot] = jnp.zeros(buffer.shape[1:], buffer.dtype)

    G = jnp.zeros((4 * KL, 128), F)
    lower_y, upper_y = range(0, half, 2), range(half, CY, 2)
    fetch[3, 0].wait()
    stage(3, None, G, lower_y)

    @pl.when(has["xm"])
    def _():
        pl.semaphore_wait(barrier, peers)
        pl.semaphore_signal(ready, inc=1, device_id=beside["xm"], device_id_type=MESH)

    fetch[0, 1].wait()
    stage(0, None, G, upper_y)
    start("xm", x_down)

    @pl.when(has["xm"] & has["xp"])
    def _():
        pl.semaphore_wait(ready, 1)
        x_up.start()

    fetch[3, 1].wait()
    stage(3, None, G, upper_y)
    fetch[0, 0].wait()
    stage(0, None, G, lower_y)
    fetch[2, None].wait()
    fetch_s.wait()
    G = stage(2, 3, G)

    @pl.when(jnp.logical_not(has["xm"]))
    def _():
        pl.semaphore_wait(barrier, peers)

    @pl.when(jnp.logical_not(has["xm"]) & jnp.logical_not(line0))
    def _():
        pl.semaphore_wait(ready, 1)
        x_up.start()

    fetch[1, None].wait()
    for x in range(CX):
        low = m[x, :, 0:16, :].astype(F)[:, 0, :]
        high = m[x, :, CZ - 16 : CZ, :].astype(F)[:, 15, :]
        ok = live_lanes[:CY]
        zs[0, CY * x : CY * (x + 1)] = jnp.where(ok, low, 0.0).astype(BF)
        zs[1, CY * x : CY * (x + 1)] = jnp.where(ok, high, 0.0).astype(BF)
    start("zp", z_up)
    start("zm", z_down)
    G = stage(1, 2, G)
    start("yp", y_up)
    start("ym", y_down)
    G = stage(None, 1, G)
    G = stage(None, 0, G)
    G = G[: 2 * KL] + G[2 * KL :]

    def both(g):
        return jnp.where(live_lanes[:KL, :KS], g[:KL, :KS] + g[KL : 2 * KL, KS:], 0.0)

    def flip(b):
        wide = jnp.concatenate([b, jnp.zeros((KL, KS), F)], 1)
        wide = jnp.concatenate([wide, jnp.zeros((128 - KL, 128), F)], 0)
        return jnp.transpose(wide)[:KL, :KS]

    C = both(G)
    C = 0.5 * (C + flip(C))
    r48 = lax.broadcasted_iota(jnp.int32, (KL, KS), 0)
    l48 = lax.broadcasted_iota(jnp.int32, (KL, KS), 1)
    C = jnp.where((r48 == l48) & (r48 >= count), 1.0, C)

    def both_z(g):
        return -(g[:KL, :KS] + g[KS : KS + KL, KS:])

    arrived("zm", z_up, zr, 0)
    arrived("zp", z_down, zr, 1)
    zp = both_z(lax.dot_general(zs[1], zr[1], TN, preferred_element_type=F))

    mine = lead.at[jnp.minimum(gz, PSUB - 1)]
    mine_sem = lrecv.at[jnp.minimum(gz, PSUB - 1)]
    along = [remote(mine, mine, lsend.at[t], mine_sem, {"gz": t}) for t in range(PSUB + 1)]

    @pl.when(leader)
    def _():
        lead[jnp.minimum(gz, PSUB - 1)] = jnp.concatenate([C, zp], 1)
        for t in range(PSUB + 1):
            pl.when(gz != t)(along[t].start)

    @pl.when(line0)
    def _():
        pl.semaphore_wait(ready, 1)
        x_up.start()

    zmT = both_z(lax.dot_general(zr[0], zs[0], TN, preferred_element_type=F))
    zpT = both_z(lax.dot_general(zr[1], zs[1], TN, preferred_element_type=F))

    def face(tiles, own):
        left = jnp.concatenate(tiles, 1)
        right = jnp.concatenate(own, 0)
        return -both(jnp.dot(left, right, preferred_element_type=F))

    arrived("ym", y_up, yr, 0)
    arrived("yp", y_down, yr, 1)
    ymT = face([yr[0, x] for x in range(CX)], [m[x, 0] for x in range(CX)])
    ypT = face([yr[1, x] for x in range(CX)], [m[x, CY - 1] for x in range(CX)])

    def pack(k, a, b):
        gath[gz, k] = jnp.where(core == 1, jnp.concatenate([b, a], 1), jnp.concatenate([a, b], 1))

    zero = jnp.zeros((KL, KS), F)
    pack(0, C, ymT)
    pack(1, ypT, zpT)

    class Gather:
        def __init__(self, at, send, recv, steps):
            give = lambda c, t, k: remote(at(c), at(c), send.at[k], recv.at[c], {"gz": t})
            number = iter(range(15))
            self.steps = [(waits, [give(c, t, next(number)) for c, t in pairs]) for waits, pairs in steps]
            self.sends = [s for _, sends in self.steps for s in sends]
            self.wait = lambda c: remote(at(c), at(c), send.at[0], recv.at[c], {"gz": partner}).wait_recv()

        def step(self, k):
            waits, sends = self.steps[k]
            if len(waits) == len(sends):
                for c, s in zip(waits, sends):
                    self.wait(c)
                    s.start()
                return
            for c in waits:
                self.wait(c)
            for s in sends:
                s.start()

    mine_all = (gz, partner) + around + tuple(also(t) for t in around)
    of_sibling = [t + 1 - 2 * core for t in mine_all]
    far = [also(t) for t in around]
    early = Gather(
        lambda c: gath.at[c, pl.ds(0, 2)], esend, erecv,
        [
            ([], [(gz, t) for t in (partner,) + around + (sibling,)]),
            ([partner], [(partner, t) for t in around + (sibling,)]),
            (list(around), [(t, sibling) for t in around]),
            (far, [(t, sibling) for t in far]),
            (of_sibling, []),
        ],
    )
    late = Gather(
        lambda c: gath.at[c, 2], rsend, rrecv,
        [
            ([], [(gz, t) for t in (partner,) + around + tuple(far) + (sibling,)]),
            ([partner] + list(around) + far, [(t, sibling) for t in [partner] + list(around) + far]),
            (of_sibling, []),
        ],
    )
    early.step(0)

    eye = jnp.where(r48 == l48, 1.0, 0.0)
    for i in range(PSUB):
        b = jnp.where(gz == i, C, zero)
        b = jnp.where(gz == i - 1, zpT, b)
        b = jnp.where(gz == i + 1, zmT, b)
        rhs[i] = jnp.concatenate([b, jnp.where(gz == i, eye, zero)], 1)
        xs[i] = jnp.zeros((KL, 128), F)
    sub[...] = jnp.zeros((KL, 256), F)

    r16 = lax.broadcasted_iota(jnp.int32, (KS - KL, NGZ * KS), 0) + KL
    l16 = lax.rem(lax.broadcasted_iota(jnp.int32, (KS - KL, NGZ * KS), 1), KS)
    out[KL:KS, :] = jnp.where(r16 == l16, 1.0, 0.0)
    for b in range(1, 7):
        out[KS * b + KL : KS * (b + 1), :] = jnp.zeros((KS - KL, NGZ * KS), F)

    first_lanes = lax.broadcasted_iota(jnp.int32, (KL, 128), 1) < KS

    def step(i, _):
        @pl.when(gz != i)
        def _():
            remote(lead.at[i], lead.at[i], lsend.at[0], lrecv.at[i], {"gz": partner}).wait_recv()

        g = sub[...]
        a1 = lead[i] - jnp.where(first_lanes, g[:, :128], 0.0)
        a2 = rhs[i] - g[:, 128:]
        A = eliminate([[a1[8 * k : 8 * k + 8], a2[8 * k : 8 * k + 8]] for k in range(KL // 8)])
        a1 = jnp.concatenate([a[0] for a in A], 0)
        a2 = jnp.concatenate([a[1] for a in A], 0)
        xs[i] = a2
        turned = pltpu.roll(a1, KS, 1)
        sub[...] = outer_gram(turned[:, :KS], jnp.concatenate([turned, a2], 1))[:KL]
        return 0

    def chain(low, high):
        @pl.when(chained)
        def _():
            lax.fori_loop(low, high, step, 0)

    early.step(1)
    chain(0, 2)
    early.step(2)
    arrived("xm", x_up, xr, 0)
    low = face([xr[0, y] for y in range(half)], [m[0, y] for y in range(half)])
    part[0] = jnp.concatenate([flip(low), zero], 1)
    start("xm", p_down)
    arrived("xp", x_down, xr, 1)
    high = face([xr[1, y] for y in range(half)], [m[CX - 1, half + y] for y in range(half)])
    part[1] = jnp.concatenate([flip(high), zero], 1)
    start("xp", p_up)
    chain(2, 6)
    early.step(3)
    arrived("xm", p_up, partr, 0)
    arrived("xp", p_down, partr, 1)
    xpT = high + partr[1, :, :KS]
    pack(2, low + partr[0, :, :KS], xpT)
    late.step(0)
    chain(6, PSUB)

    to_y = remote(post.at[0], postr, osend.at[0], orecv, beside["yp"])
    to_x = remote(post.at[1], postr, osend.at[1], orecv, beside["xp"])

    @pl.when(leader)
    def _():
        right = jnp.concatenate([flip(ypT), flip(xpT)], 1)
        wide = [
            jnp.dot(xs[i][:, KS : KS + KL], right, precision=lax.Precision.HIGHEST, preferred_element_type=F)
            for i in range(PSUB)
        ]
        for p in range(PSUB // 2):
            a, b = wide[2 * p], wide[2 * p + 1]
            post[0, p] = jnp.concatenate([a[:, :KS], b[:, :KS]], 1)
            post[1, p] = jnp.concatenate([a[:, KS:], b[:, KS:]], 1)
        to_y.start()
        to_x.start()


    @pl.when(chained)
    def _():
        late.step(1)

    left = lax.broadcasted_iota(jnp.int32, (KL, 128), 1) < KS

    def lay(p, k, a, b):
        first, second = gath[2 * p, k], gath[2 * p + 1, k]
        cols = slice(128 * p, 128 * (p + 1))
        out[KS * a : KS * a + KL, cols] = jnp.where(left, first, second)
        out[KS * b : KS * b + KL, cols] = pltpu.roll(jnp.where(left, second, first), KS, 1)

    early.step(4)
    for p in range(NGZ // 2):
        lay(p, 0, 0, 3)
        lay(p, 1, 4, 6)
        below = gath[2 * p - 1, 1] if p > 0 else jnp.zeros((KL, 128), F)
        both_below = jnp.where(left, below, gath[2 * p, 1])
        turned = jnp.transpose(jnp.concatenate([both_below, jnp.zeros((128 - KL, 128), F)], 0))
        out[KS * 5 : KS * 5 + KL, 128 * p : 128 * (p + 1)] = jnp.concatenate(
            [turned[:KL, :KS], turned[KS : KS + KL, :KS]], 1
        )

    def put_panel(p, tile, ends):
        t = jnp.transpose(jnp.concatenate([tile, jnp.zeros((128 - KL, 128), F)], 0))
        panel_ref[:, 128 * p : 128 * (p + 1)] = jnp.concatenate([t[:KS, :KS], t[KS:, :KS]], 1) + ends

    panel_ref[...] = jnp.zeros((KS, PSUB * KS), F)

    @pl.when(chained)
    def _():
        r64 = lax.broadcasted_iota(jnp.int32, (KS, KS), 0)
        l64 = lax.broadcasted_iota(jnp.int32, (KS, KS), 1)
        dead = jnp.where((r64 == l64) & (r64 >= KL), 1.0, 0.0)
        for p in range(PSUB // 2):
            ends = [jnp.where(gz == 2 * p + k, dead, jnp.zeros((KS, KS), F)) for k in range(2)]
            tile = jnp.concatenate([xs[2 * p][:, :KS], xs[2 * p + 1][:, :KS]], 1)
            put_panel(p, tile, jnp.concatenate(ends, 1))

    @pl.when(jnp.logical_not(chained))
    def _():
        late.step(1)

    late.step(2)
    for p in range(NGZ // 2):
        lay(p, 2, 1, 2)

    @pl.when(follower)
    def _():
        to_y.wait_recv()
        for p in range(PSUB // 2):
            put_panel(p, postr[p], 0.0)

    for s in early.sends + late.sends:
        s.wait_send()
    for side, copy in ways:
        @pl.when(has[side])
        def _():
            copy.wait_send()

    @pl.when(leader)
    def _():
        to_y.wait_send()
        to_x.wait_send()
        for t in range(PSUB + 1):
            pl.when(gz != t)(along[t].wait_send)


def local(vectors, diag_shift, coupling, counts):
    dma = pltpu.SemaphoreType.DMA
    columns, panel = pl.pallas_call(
        kernel,
        out_shape=(
            jax.ShapeDtypeStruct((7 * KS, NGZ * KS), F),
            jax.ShapeDtypeStruct((KS, PSUB * KS), F),
        ),
        in_specs=[pl.BlockSpec(memory_space=pltpu.SMEM)] + [pl.BlockSpec(memory_space=pltpu.HBM)] * 2,
        out_specs=(pl.BlockSpec(memory_space=pltpu.VMEM), pl.BlockSpec(memory_space=pltpu.VMEM)),
        scratch_shapes=[
            pltpu.VMEM((CX, CY, CZ, 128), BF),
            pltpu.VMEM((CX, CY, 2 * KL, CZ), BF),
            pltpu.VMEM((3, CX, CY, CZ), F),
            pltpu.VMEM((2, CY // 2, 2 * KL, CZ), BF),
            pltpu.VMEM((2, CX, 2 * KL, CZ), BF),
            pltpu.VMEM((2, CX * CY, 128), BF),
            pltpu.VMEM((2, CX * CY, 128), BF),
            pltpu.VMEM((2, KL, 128), F),
            pltpu.VMEM((2, KL, 128), F),
            pltpu.VMEM((PSUB, KL, 128), F),
            pltpu.VMEM((PSUB, KL, 128), F),
            pltpu.VMEM((PSUB, KL, 128), F),
            pltpu.VMEM((KL, 256), F),
            pltpu.VMEM((NGZ, 3, KL, 128), F),
            pltpu.VMEM((2, PSUB // 2, KL, 128), F),
            pltpu.VMEM((PSUB // 2, KL, 128), F),
            pltpu.SemaphoreType.REGULAR,
            dma((7,)),
            dma((2,)), dma((2,)), dma((2,)), dma((2,)), dma((2,)), dma((2,)), dma((2,)), dma((2,)),
            dma((PSUB + 1,)), dma((PSUB,)), dma((2,)), dma, dma((15,)), dma((NGZ,)), dma((15,)), dma((NGZ,)),
        ],
        compiler_params=pltpu.CompilerParams(
            collective_id=0, has_side_effects=True, vmem_limit_bytes=(50 << 20) + (100 << 10)
        ),
    )(counts, vectors, jnp.concatenate([diag_shift, coupling[None]], 0))
    return columns.T, panel


def solution(mesh):
    return jax.shard_map(
        local,
        mesh=mesh,
        in_specs=(
            P("gx", "gy", "gz", None),
            P(None, "gx", "gy", "gz"),
            P("gx", "gy", "gz"),
            P(("gx", "gy", "gz")),
        ),
        out_specs=(P(("gx", "gy"), None), P(("gx", "gy", "gz"), None)),
        check_vma=False,
    )
```

```python
import jax
import jax.numpy as jnp
from jax import lax
from jax.experimental import pallas as pl
from jax.experimental.pallas import tpu as pltpu
from jax.sharding import PartitionSpec as P

F = jnp.float32
BF = jnp.bfloat16
CX, CY, CZ = 4, 16, 128
KS = 64
KL = 48
PSUB = 8
NGX, NGY, NGZ = 4, 4, 16
GROUP = 16
MESH = pl.DeviceIdType.MESH


def remote(src, dst, send, recv, device):
    return pltpu.make_async_remote_copy(
        src_ref=src, dst_ref=dst, send_sem=send, recv_sem=recv, device_id=device, device_id_type=MESH
    )


def lanes_of(x, c):
    return jnp.broadcast_to(x[:, c : c + 1], (8, 128))


def rows_of(x, r):
    return jnp.broadcast_to(x[r : r + 1, :], (8, 128))


def eliminate(A):
    rows = lax.broadcasted_iota(jnp.int32, (8, 128), 0)
    n = KL // 8
    for first in range(0, KL, GROUP):
        copies = [[None] * n for _ in range(GROUP)]
        for c in range(GROUP):
            for i in range(first // 8, n):
                copies[c][i] = lanes_of(A[i][0], first + c)
        p = rows_of(copies[0][first // 8], 0)
        for c in range(GROUP):
            J, s = (first + c) // 8, c % 8
            if c + 1 < GROUP:
                ahead = rows_of(copies[c + 1][(first + c + 1) // 8], (c + 1) % 8)
            r = lax.rsqrt(p)
            row = [rows_of(a, s) * r for a in A[J]]
            beside = [rows_of(copies[k][J], s) * r for k in range(c + 1, GROUP)]
            if c + 1 < GROUP:
                p = ahead - beside[0] * beside[0]
            for i in range(J, n):
                f = copies[c][i] * r
                if i == J:
                    f = jnp.where(rows > s, f, 0.0)
                for q in range(len(row)):
                    A[i][q] = A[i][q] - f * row[q]
                for k in range(c + 1, GROUP):
                    copies[k][i] = copies[k][i] - f * beside[k - c - 1]
            for q in range(len(row)):
                A[J][q] = jnp.where(rows == s, row[q], A[J][q])
    return A


def split3(x):
    h = x.astype(BF)
    x = x - h.astype(F)
    m = x.astype(BF)
    x = x - m.astype(F)
    return h, m, x.astype(BF)


TN = (((0,), (0,)), ((), ()))


def outer_gram(W, X):
    wh, wm, wl = split3(W)
    h, m, low = split3(X)
    left1, right1 = jnp.concatenate([wh, wh, wm], 0), jnp.concatenate([h, m, h], 0)
    left2, right2 = jnp.concatenate([wm, wh, wl], 0), jnp.concatenate([m, low, h], 0)
    return lax.dot_general(left1, right1, TN, preferred_element_type=F) + lax.dot_general(
        left2, right2, TN, preferred_element_type=F
    )


def kernel(
    cnt_ref, m_hbm, s_hbm, out, panel_ref,
    m, tt, sh, xr, yr, zs, zr, part, partr, lead, rhs, xs, sub, gath, post, postr,
    ready, load, xsend, xrecv, ysend, yrecv, zsend, zrecv, psend, precv, lsend, lrecv, osend, orecv, esend, erecv, rsend, rrecv,
):
    gx, gy, gz = lax.axis_index("gx"), lax.axis_index("gy"), lax.axis_index("gz")
    has = {
        "xm": gx > 0, "xp": gx < NGX - 1,
        "ym": gy > 0, "yp": gy < NGY - 1,
        "zm": gz > 0, "zp": gz < NGZ - 1,
    }
    beside = {
        "xm": {"gx": gx - 1}, "xp": {"gx": gx + 1},
        "ym": {"gy": gy - 1}, "yp": {"gy": gy + 1},
        "zm": {"gz": gz - 1}, "zp": {"gz": gz + 1},
    }
    barrier = pltpu.get_barrier_semaphore()
    core = lax.rem(gz, 2)
    partner = lax.rem(gz + 8, NGZ)
    sibling = gz + 1 - 2 * core
    plane = 8 * (gz // 8)
    ring = lambda k: plane + lax.rem(gz - plane + 2 * k, 8)
    up, opposite, down = ring(1), ring(2), ring(3)
    line0 = (gx == 0) & (gy == 0)
    line_y = (gx == 0) & (gy == 1)
    line_x = (gx == 1) & (gy == 0)
    leader = line0 & (gz < PSUB)
    chained = line0 & (gz <= PSUB)
    follower = (line_y | line_x) & (gz < PSUB)

    also = lambda c: lax.rem(c + 8, NGZ)
    around = (up, down, opposite)
    for t in (partner, sibling) + around + tuple(also(t) for t in around):
        pl.semaphore_signal(barrier, inc=1, device_id={"gz": t}, device_id_type=MESH)
    peers = 8
    for side, other in (("xp", "xm"), ("ym", "ym"), ("yp", "yp"), ("zm", "zm"), ("zp", "zp")):
        @pl.when(has[side])
        def _():
            pl.semaphore_signal(barrier, inc=1, device_id=beside[side], device_id_type=MESH)

        peers = peers + has[other].astype(jnp.int32)
    for t in range(PSUB):
        @pl.when(chained & (gz != t))
        def _():
            pl.semaphore_signal(barrier, inc=1, device_id={"gz": t}, device_id_type=MESH)
    peers = peers + jnp.where(leader, PSUB, 0)

    half = CY // 2
    fetch = {}
    for k, (x, h) in enumerate([(3, 0), (0, 1), (3, 1), (0, 0), (2, None), (1, None)]):
        part_of = (x,) if h is None else (x, pl.ds(half * h, half))
        fetch[x, h] = pltpu.make_async_copy(m_hbm.at[part_of], m.at[part_of], load.at[k])
        fetch[x, h].start()
    fetch_s = pltpu.make_async_copy(s_hbm, sh, load.at[6])
    fetch_s.start()

    count = cnt_ref[0]
    r128 = lax.broadcasted_iota(jnp.int32, (128, 128), 0)
    l128 = lax.broadcasted_iota(jnp.int32, (128, 128), 1)
    live_rows = (jnp.where(r128 >= KS, r128 - KS, r128) < count).astype(F).astype(BF)
    live_lanes = (jnp.where(l128 >= KS, l128 - KS, l128) < count)[:KS]

    inner_z = jnp.where(lax.broadcasted_iota(jnp.int32, (KL, 128), 1) < CZ - 1, 1.0, 0.0)

    def transpose(x, y):
        t = jnp.swapaxes(m[x, y], 0, 1) * live_rows
        tt[x, y, 0:KL] = t[0:KL]
        tt[x, y, KL : 2 * KL] = t[KS : KS + KL]

    def image(x, y):
        wide = (KL, 128)
        a0 = jnp.broadcast_to(sh[0, x, y : y + 1, :] + 6.0, wide)
        a1 = jnp.broadcast_to(sh[1, x, y : y + 1, :] + 6.0, wide)
        c = jnp.broadcast_to(sh[2, x, y : y + 1, :], wide)
        u = tt[x, y, 0:KL, :].astype(F)
        v = tt[x, y, KL : 2 * KL, :].astype(F)

        def forward(w, at):
            n = pltpu.roll(w, CZ - 1, 1) * inner_z
            if y < CY - 1:
                n = n + tt[x, y + 1, at : at + KL, :].astype(F)
            if x < CX - 1:
                n = n + tt[x + 1, y, at : at + KL, :].astype(F)
            return n

        yu = a0 * u + c * v - 2.0 * forward(u, 0)
        yv = a1 * v + c * u - 2.0 * forward(v, KL)
        high = [w.astype(BF) for w in (yu, yv)]
        return jnp.concatenate(high + [(w - h.astype(F)).astype(BF) for w, h in zip((yu, yv), high)], 0)

    def stage(tx, yx, G, ys=range(0, CY, 2)):
        for y in ys:
            if tx is not None:
                transpose(tx, y)
                transpose(tx, y + 1)
            if yx is not None:
                left = jnp.concatenate([image(yx, y), image(yx, y + 1)], 1)
                right = jnp.concatenate([m[yx, y], m[yx, y + 1]], 0)
                G = G + jnp.dot(left, right, preferred_element_type=F)
        return G

    x_up = remote(tt.at[3, pl.ds(0, half)], xr.at[0], xsend.at[0], xrecv.at[0], beside["xp"])
    x_down = remote(tt.at[0, pl.ds(half, half)], xr.at[1], xsend.at[1], xrecv.at[1], beside["xm"])
    y_up = remote(tt.at[:, CY - 1], yr.at[0], ysend.at[0], yrecv.at[0], beside["yp"])
    y_down = remote(tt.at[:, 0], yr.at[1], ysend.at[1], yrecv.at[1], beside["ym"])
    z_up = remote(zs.at[1], zr.at[0], zsend.at[0], zrecv.at[0], beside["zp"])
    z_down = remote(zs.at[0], zr.at[1], zsend.at[1], zrecv.at[1], beside["zm"])
    p_up = remote(part.at[1], partr.at[0], psend.at[0], precv.at[0], beside["xp"])
    p_down = remote(part.at[0], partr.at[1], psend.at[1], precv.at[1], beside["xm"])
    ways = [
        ("xp", x_up), ("xm", x_down), ("yp", y_up), ("ym", y_down),
        ("zp", z_up), ("zm", z_down), ("xp", p_up), ("xm", p_down),
    ]

    def start(side, copy):
        @pl.when(has[side])
        def _():
            copy.start()

    def arrived(side, copy, buffer, slot):
        @pl.when(has[side])
        def _():
            copy.wait_recv()

        @pl.when(jnp.logical_not(has[side]))
        def _():
            buffer[slot] = jnp.zeros(buffer.shape[1:], buffer.dtype)

    G = jnp.zeros((4 * KL, 128), F)
    lower_y, upper_y = range(0, half, 2), range(half, CY, 2)
    fetch[3, 0].wait()
    stage(3, None, G, lower_y)

    @pl.when(has["xm"])
    def _():
        pl.semaphore_wait(barrier, peers)
        pl.semaphore_signal(ready, inc=1, device_id=beside["xm"], device_id_type=MESH)

    fetch[0, 1].wait()
    stage(0, None, G, upper_y)
    start("xm", x_down)

    @pl.when(has["xm"] & has["xp"])
    def _():
        pl.semaphore_wait(ready, 1)
        x_up.start()

    fetch[3, 1].wait()
    stage(3, None, G, upper_y)
    fetch[0, 0].wait()
    stage(0, None, G, lower_y)
    fetch[2, None].wait()
    fetch_s.wait()
    G = stage(2, 3, G)

    @pl.when(jnp.logical_not(has["xm"]))
    def _():
        pl.semaphore_wait(barrier, peers)

    fetch[1, None].wait()
    for x in range(CX):
        low = m[x, :, 0:16, :].astype(F)[:, 0, :]
        high = m[x, :, CZ - 16 : CZ, :].astype(F)[:, 15, :]
        ok = live_lanes[:CY]
        zs[0, CY * x : CY * (x + 1)] = jnp.where(ok, low, 0.0).astype(BF)
        zs[1, CY * x : CY * (x + 1)] = jnp.where(ok, high, 0.0).astype(BF)
    start("zp", z_up)
    start("zm", z_down)
    G = stage(1, 2, G)
    start("yp", y_up)
    start("ym", y_down)
    G = stage(None, 1, G)
    G = stage(None, 0, G)
    G = G[: 2 * KL] + G[2 * KL :]

    def both(g):
        return jnp.where(live_lanes[:KL, :KS], g[:KL, :KS] + g[KL : 2 * KL, KS:], 0.0)

    def flip(b):
        wide = jnp.concatenate([b, jnp.zeros((KL, KS), F)], 1)
        wide = jnp.concatenate([wide, jnp.zeros((128 - KL, 128), F)], 0)
        return jnp.transpose(wide)[:KL, :KS]

    C = both(G)
    C = 0.5 * (C + flip(C))
    r48 = lax.broadcasted_iota(jnp.int32, (KL, KS), 0)
    l48 = lax.broadcasted_iota(jnp.int32, (KL, KS), 1)
    C = jnp.where((r48 == l48) & (r48 >= count), 1.0, C)

    def both_z(g):
        return -(g[:KL, :KS] + g[KS : KS + KL, KS:])

    arrived("zm", z_up, zr, 0)
    arrived("zp", z_down, zr, 1)
    zp = both_z(lax.dot_general(zs[1], zr[1], TN, preferred_element_type=F))

    mine = lead.at[jnp.minimum(gz, PSUB - 1)]
    mine_sem = lrecv.at[jnp.minimum(gz, PSUB - 1)]
    along = [remote(mine, mine, lsend.at[t], mine_sem, {"gz": t}) for t in range(PSUB + 1)]

    @pl.when(leader)
    def _():
        lead[jnp.minimum(gz, PSUB - 1)] = jnp.concatenate([C, zp], 1)
        for t in range(PSUB + 1):
            pl.when(gz != t)(along[t].start)

    @pl.when(jnp.logical_not(has["xm"]))
    def _():
        pl.semaphore_wait(ready, 1)
        x_up.start()

    zmT = both_z(lax.dot_general(zr[0], zs[0], TN, preferred_element_type=F))
    zpT = both_z(lax.dot_general(zr[1], zs[1], TN, preferred_element_type=F))

    def face(tiles, own):
        left = jnp.concatenate(tiles, 1)
        right = jnp.concatenate(own, 0)
        return -both(jnp.dot(left, right, preferred_element_type=F))

    arrived("ym", y_up, yr, 0)
    arrived("yp", y_down, yr, 1)
    ymT = face([yr[0, x] for x in range(CX)], [m[x, 0] for x in range(CX)])
    ypT = face([yr[1, x] for x in range(CX)], [m[x, CY - 1] for x in range(CX)])

    def pack(k, a, b):
        gath[gz, k] = jnp.where(core == 1, jnp.concatenate([b, a], 1), jnp.concatenate([a, b], 1))

    zero = jnp.zeros((KL, KS), F)
    pack(0, C, ymT)
    pack(1, ypT, zpT)

    class Gather:
        def __init__(self, at, send, recv, steps):
            give = lambda c, t, k: remote(at(c), at(c), send.at[k], recv.at[c], {"gz": t})
            number = iter(range(15))
            self.steps = [(waits, [give(c, t, next(number)) for c, t in pairs]) for waits, pairs in steps]
            self.sends = [s for _, sends in self.steps for s in sends]
            self.wait = lambda c: remote(at(c), at(c), send.at[0], recv.at[c], {"gz": partner}).wait_recv()

        def step(self, k):
            waits, sends = self.steps[k]
            if len(waits) == len(sends):
                for c, s in zip(waits, sends):
                    self.wait(c)
                    s.start()
                return
            for c in waits:
                self.wait(c)
            for s in sends:
                s.start()

    mine_all = (gz, partner) + around + tuple(also(t) for t in around)
    of_sibling = [t + 1 - 2 * core for t in mine_all]
    far = [also(t) for t in around]
    early = Gather(
        lambda c: gath.at[c, pl.ds(0, 2)], esend, erecv,
        [
            ([], [(gz, t) for t in (partner,) + around + (sibling,)]),
            ([partner], [(partner, t) for t in around + (sibling,)]),
            (list(around), [(t, sibling) for t in around]),
            (far, [(t, sibling) for t in far]),
            (of_sibling, []),
        ],
    )
    late = Gather(
        lambda c: gath.at[c, 2], rsend, rrecv,
        [
            ([], [(gz, t) for t in tuple(far) + around + (partner, sibling)]),
            ([partner] + list(around) + far, [(t, sibling) for t in [partner] + list(around) + far]),
            (of_sibling, []),
        ],
    )
    early.step(0)

    eye = jnp.where(r48 == l48, 1.0, 0.0)
    for i in range(PSUB):
        b = jnp.where(gz == i, C, zero)
        b = jnp.where(gz == i - 1, zpT, b)
        b = jnp.where(gz == i + 1, zmT, b)
        rhs[i] = jnp.concatenate([b, jnp.where(gz == i, eye, zero)], 1)
        xs[i] = jnp.zeros((KL, 128), F)
    sub[...] = jnp.zeros((KL, 256), F)

    r16 = lax.broadcasted_iota(jnp.int32, (KS - KL, NGZ * KS), 0) + KL
    l16 = lax.rem(lax.broadcasted_iota(jnp.int32, (KS - KL, NGZ * KS), 1), KS)
    out[KL:KS, :] = jnp.where(r16 == l16, 1.0, 0.0)
    for b in range(1, 7):
        out[KS * b + KL : KS * (b + 1), :] = jnp.zeros((KS - KL, NGZ * KS), F)

    first_lanes = lax.broadcasted_iota(jnp.int32, (KL, 128), 1) < KS

    def step(i, _):
        @pl.when(gz != i)
        def _():
            remote(lead.at[i], lead.at[i], lsend.at[0], lrecv.at[i], {"gz": partner}).wait_recv()

        g = sub[...]
        a1 = lead[i] - jnp.where(first_lanes, g[:, :128], 0.0)
        a2 = rhs[i] - g[:, 128:]
        A = eliminate([[a1[8 * k : 8 * k + 8], a2[8 * k : 8 * k + 8]] for k in range(KL // 8)])
        a1 = jnp.concatenate([a[0] for a in A], 0)
        a2 = jnp.concatenate([a[1] for a in A], 0)
        xs[i] = a2
        turned = pltpu.roll(a1, KS, 1)
        sub[...] = outer_gram(turned[:, :KS], jnp.concatenate([turned, a2], 1))[:KL]
        return 0

    def chain(low, high):
        @pl.when(chained)
        def _():
            lax.fori_loop(low, high, step, 0)

    early.step(1)
    chain(0, 2)
    early.step(2)
    arrived("xm", x_up, xr, 0)
    low = face([xr[0, y] for y in range(half)], [m[0, y] for y in range(half)])
    part[0] = jnp.concatenate([flip(low), zero], 1)
    start("xm", p_down)
    arrived("xp", x_down, xr, 1)
    high = face([xr[1, y] for y in range(half)], [m[CX - 1, half + y] for y in range(half)])
    part[1] = jnp.concatenate([flip(high), zero], 1)
    start("xp", p_up)
    chain(2, 5)
    arrived("xm", p_up, partr, 0)
    arrived("xp", p_down, partr, 1)
    xpT = high + partr[1, :, :KS]
    pack(2, low + partr[0, :, :KS], xpT)
    late.step(0)
    early.step(3)
    chain(5, PSUB)

    to_y = remote(post.at[0], postr, osend.at[0], orecv, beside["yp"])
    to_x = remote(post.at[1], postr, osend.at[1], orecv, beside["xp"])

    @pl.when(leader)
    def _():
        right = jnp.concatenate([flip(ypT), flip(xpT)], 1)
        wide = [
            jnp.dot(xs[i][:, KS : KS + KL], right, precision=lax.Precision.HIGHEST, preferred_element_type=F)
            for i in range(PSUB)
        ]
        for p in range(PSUB // 2):
            a, b = wide[2 * p], wide[2 * p + 1]
            post[0, p] = jnp.concatenate([a[:, :KS], b[:, :KS]], 1)
            post[1, p] = jnp.concatenate([a[:, KS:], b[:, KS:]], 1)
        to_y.start()
        to_x.start()


    left = lax.broadcasted_iota(jnp.int32, (KL, 128), 1) < KS

    def lay(p, k, a, b):
        first, second = gath[2 * p, k], gath[2 * p + 1, k]
        cols = slice(128 * p, 128 * (p + 1))
        out[KS * a : KS * a + KL, cols] = jnp.where(left, first, second)
        out[KS * b : KS * b + KL, cols] = pltpu.roll(jnp.where(left, second, first), KS, 1)

    early.step(4)
    for p in range(NGZ // 2):
        lay(p, 0, 0, 3)
        lay(p, 1, 4, 6)
        below = gath[2 * p - 1, 1] if p > 0 else jnp.zeros((KL, 128), F)
        both_below = jnp.where(left, below, gath[2 * p, 1])
        turned = jnp.transpose(jnp.concatenate([both_below, jnp.zeros((128 - KL, 128), F)], 0))
        out[KS * 5 : KS * 5 + KL, 128 * p : 128 * (p + 1)] = jnp.concatenate(
            [turned[:KL, :KS], turned[KS : KS + KL, :KS]], 1
        )

    def put_panel(p, tile, ends):
        t = jnp.transpose(jnp.concatenate([tile, jnp.zeros((128 - KL, 128), F)], 0))
        panel_ref[:, 128 * p : 128 * (p + 1)] = jnp.concatenate([t[:KS, :KS], t[KS:, :KS]], 1) + ends

    panel_ref[...] = jnp.zeros((KS, PSUB * KS), F)

    @pl.when(chained)
    def _():
        r64 = lax.broadcasted_iota(jnp.int32, (KS, KS), 0)
        l64 = lax.broadcasted_iota(jnp.int32, (KS, KS), 1)
        dead = jnp.where((r64 == l64) & (r64 >= KL), 1.0, 0.0)
        for p in range(PSUB // 2):
            ends = [jnp.where(gz == 2 * p + k, dead, jnp.zeros((KS, KS), F)) for k in range(2)]
            tile = jnp.concatenate([xs[2 * p][:, :KS], xs[2 * p + 1][:, :KS]], 1)
            put_panel(p, tile, jnp.concatenate(ends, 1))

    late.step(1)
    late.step(2)
    for p in range(NGZ // 2):
        lay(p, 2, 1, 2)

    @pl.when(follower)
    def _():
        to_y.wait_recv()
        for p in range(PSUB // 2):
            put_panel(p, postr[p], 0.0)

    for s in early.sends + late.sends:
        s.wait_send()
    for side, copy in ways:
        @pl.when(has[side])
        def _():
            copy.wait_send()

    @pl.when(leader)
    def _():
        to_y.wait_send()
        to_x.wait_send()
        for t in range(PSUB + 1):
            pl.when(gz != t)(along[t].wait_send)


def local(vectors, diag_shift, coupling, counts):
    dma = pltpu.SemaphoreType.DMA
    columns, panel = pl.pallas_call(
        kernel,
        out_shape=(
            jax.ShapeDtypeStruct((7 * KS, NGZ * KS), F),
            jax.ShapeDtypeStruct((KS, PSUB * KS), F),
        ),
        in_specs=[pl.BlockSpec(memory_space=pltpu.SMEM)] + [pl.BlockSpec(memory_space=pltpu.HBM)] * 2,
        out_specs=(pl.BlockSpec(memory_space=pltpu.VMEM), pl.BlockSpec(memory_space=pltpu.VMEM)),
        scratch_shapes=[
            pltpu.VMEM((CX, CY, CZ, 128), BF),
            pltpu.VMEM((CX, CY, 2 * KL, CZ), BF),
            pltpu.VMEM((3, CX, CY, CZ), F),
            pltpu.VMEM((2, CY // 2, 2 * KL, CZ), BF),
            pltpu.VMEM((2, CX, 2 * KL, CZ), BF),
            pltpu.VMEM((2, CX * CY, 128), BF),
            pltpu.VMEM((2, CX * CY, 128), BF),
            pltpu.VMEM((2, KL, 128), F),
            pltpu.VMEM((2, KL, 128), F),
            pltpu.VMEM((PSUB, KL, 128), F),
            pltpu.VMEM((PSUB, KL, 128), F),
            pltpu.VMEM((PSUB, KL, 128), F),
            pltpu.VMEM((KL, 256), F),
            pltpu.VMEM((NGZ, 3, KL, 128), F),
            pltpu.VMEM((2, PSUB // 2, KL, 128), F),
            pltpu.VMEM((PSUB // 2, KL, 128), F),
            pltpu.SemaphoreType.REGULAR,
            dma((7,)),
            dma((2,)), dma((2,)), dma((2,)), dma((2,)), dma((2,)), dma((2,)), dma((2,)), dma((2,)),
            dma((PSUB + 1,)), dma((PSUB,)), dma((2,)), dma, dma((15,)), dma((NGZ,)), dma((15,)), dma((NGZ,)),
        ],
        compiler_params=pltpu.CompilerParams(
            collective_id=0, has_side_effects=True, vmem_limit_bytes=(50 << 20) + (100 << 10)
        ),
    )(counts, vectors, jnp.concatenate([diag_shift, coupling[None]], 0))
    return columns.T, panel


def solution(mesh):
    return jax.shard_map(
        local,
        mesh=mesh,
        in_specs=(
            P("gx", "gy", "gz", None),
            P(None, "gx", "gy", "gz"),
            P("gx", "gy", "gz"),
            P(("gx", "gy", "gz")),
        ),
        out_specs=(P(("gx", "gy"), None), P(("gx", "gy", "gz"), None)),
        check_vma=False,
    )
```

```python
import jax
import jax.numpy as jnp
from jax import lax
from jax.experimental import pallas as pl
from jax.experimental.pallas import tpu as pltpu
from jax.sharding import PartitionSpec as P

F = jnp.float32
BF = jnp.bfloat16
CX, CY, CZ = 4, 16, 128
KS = 64
KL = 48
PSUB = 8
NGX, NGY, NGZ = 4, 4, 16
GROUP = 16
MESH = pl.DeviceIdType.MESH


def remote(src, dst, send, recv, device):
    return pltpu.make_async_remote_copy(
        src_ref=src, dst_ref=dst, send_sem=send, recv_sem=recv, device_id=device, device_id_type=MESH
    )


def lanes_of(x, c):
    return jnp.broadcast_to(x[:, c : c + 1], (8, 128))


def rows_of(x, r):
    return jnp.broadcast_to(x[r : r + 1, :], (8, 128))


def eliminate(A):
    rows = lax.broadcasted_iota(jnp.int32, (8, 128), 0)
    n = KL // 8
    for first in range(0, KL, GROUP):
        copies = [[None] * n for _ in range(GROUP)]
        for c in range(GROUP):
            for i in range(first // 8, n):
                copies[c][i] = lanes_of(A[i][0], first + c)
        p = rows_of(copies[0][first // 8], 0)
        for c in range(GROUP):
            J, s = (first + c) // 8, c % 8
            if c + 1 < GROUP:
                ahead = rows_of(copies[c + 1][(first + c + 1) // 8], (c + 1) % 8)
            r = lax.rsqrt(p)
            row = [rows_of(a, s) * r for a in A[J]]
            beside = [rows_of(copies[k][J], s) * r for k in range(c + 1, GROUP)]
            if c + 1 < GROUP:
                p = ahead - beside[0] * beside[0]
            for i in range(J, n):
                f = copies[c][i] * r
                if i == J:
                    f = jnp.where(rows > s, f, 0.0)
                for q in range(len(row)):
                    A[i][q] = A[i][q] - f * row[q]
                for k in range(c + 1, GROUP):
                    copies[k][i] = copies[k][i] - f * beside[k - c - 1]
            for q in range(len(row)):
                A[J][q] = jnp.where(rows == s, row[q], A[J][q])
    return A


def split3(x):
    h = x.astype(BF)
    x = x - h.astype(F)
    m = x.astype(BF)
    x = x - m.astype(F)
    return h, m, x.astype(BF)


TN = (((0,), (0,)), ((), ()))


def outer_gram(W, X):
    wh, wm, wl = split3(W)
    h, m, low = split3(X)
    left1, right1 = jnp.concatenate([wh, wh, wm], 0), jnp.concatenate([h, m, h], 0)
    left2, right2 = jnp.concatenate([wm, wh, wl], 0), jnp.concatenate([m, low, h], 0)
    return lax.dot_general(left1, right1, TN, preferred_element_type=F) + lax.dot_general(
        left2, right2, TN, preferred_element_type=F
    )


def kernel(
    cnt_ref, m_hbm, s_hbm, out, panel_ref,
    m, tt, sh, xr, yr, zs, zr, part, partr, lead, rhs, xs, sub, gath, post, postr,
    ready, load, xsend, xrecv, ysend, yrecv, zsend, zrecv, psend, precv, lsend, lrecv, osend, orecv, esend, erecv, rsend, rrecv,
):
    gx, gy, gz = lax.axis_index("gx"), lax.axis_index("gy"), lax.axis_index("gz")
    has = {
        "xm": gx > 0, "xp": gx < NGX - 1,
        "ym": gy > 0, "yp": gy < NGY - 1,
        "zm": gz > 0, "zp": gz < NGZ - 1,
    }
    beside = {
        "xm": {"gx": gx - 1}, "xp": {"gx": gx + 1},
        "ym": {"gy": gy - 1}, "yp": {"gy": gy + 1},
        "zm": {"gz": gz - 1}, "zp": {"gz": gz + 1},
    }
    barrier = pltpu.get_barrier_semaphore()
    core = lax.rem(gz, 2)
    partner = lax.rem(gz + 8, NGZ)
    sibling = gz + 1 - 2 * core
    plane = 8 * (gz // 8)
    ring = lambda k: plane + lax.rem(gz - plane + 2 * k, 8)
    up, opposite, down = ring(1), ring(2), ring(3)
    line0 = (gx == 0) & (gy == 0)
    line_y = (gx == 0) & (gy == 1)
    line_x = (gx == 1) & (gy == 0)
    leader = line0 & (gz < PSUB)
    chained = line0 & (gz <= PSUB)
    follower = (line_y | line_x) & (gz < PSUB)

    also = lambda c: lax.rem(c + 8, NGZ)
    around = (up, down, opposite)
    for t in (partner, sibling) + around + tuple(also(t) for t in around):
        pl.semaphore_signal(barrier, inc=1, device_id={"gz": t}, device_id_type=MESH)
    peers = 8
    for side, other in (("xp", "xm"), ("ym", "ym"), ("yp", "yp"), ("zm", "zm"), ("zp", "zp")):
        @pl.when(has[side])
        def _():
            pl.semaphore_signal(barrier, inc=1, device_id=beside[side], device_id_type=MESH)

        peers = peers + has[other].astype(jnp.int32)
    for t in range(PSUB):
        @pl.when(chained & (gz != t))
        def _():
            pl.semaphore_signal(barrier, inc=1, device_id={"gz": t}, device_id_type=MESH)
    peers = peers + jnp.where(leader, PSUB, 0)

    half = CY // 2
    fetch = {}
    for k, (x, h) in enumerate([(3, 0), (0, 1), (3, 1), (0, 0), (2, None), (1, None)]):
        part_of = (x,) if h is None else (x, pl.ds(half * h, half))
        fetch[x, h] = pltpu.make_async_copy(m_hbm.at[part_of], m.at[part_of], load.at[k])
        fetch[x, h].start()
    fetch_s = pltpu.make_async_copy(s_hbm, sh, load.at[6])
    fetch_s.start()

    count = cnt_ref[0]
    r128 = lax.broadcasted_iota(jnp.int32, (128, 128), 0)
    l128 = lax.broadcasted_iota(jnp.int32, (128, 128), 1)
    live_rows = (jnp.where(r128 >= KS, r128 - KS, r128) < count).astype(F).astype(BF)
    live_lanes = (jnp.where(l128 >= KS, l128 - KS, l128) < count)[:KS]

    inner_z = jnp.where(lax.broadcasted_iota(jnp.int32, (KL, 128), 1) < CZ - 1, 1.0, 0.0)

    def transpose(x, y):
        t = jnp.swapaxes(m[x, y], 0, 1) * live_rows
        tt[x, y, 0:KL] = t[0:KL]
        tt[x, y, KL : 2 * KL] = t[KS : KS + KL]

    def image(x, y):
        wide = (KL, 128)
        a0 = jnp.broadcast_to(sh[0, x, y : y + 1, :] + 6.0, wide)
        a1 = jnp.broadcast_to(sh[1, x, y : y + 1, :] + 6.0, wide)
        c = jnp.broadcast_to(sh[2, x, y : y + 1, :], wide)
        u = tt[x, y, 0:KL, :].astype(F)
        v = tt[x, y, KL : 2 * KL, :].astype(F)

        def forward(w, at):
            n = pltpu.roll(w, CZ - 1, 1) * inner_z
            if y < CY - 1:
                n = n + tt[x, y + 1, at : at + KL, :].astype(F)
            if x < CX - 1:
                n = n + tt[x + 1, y, at : at + KL, :].astype(F)
            return n

        yu = a0 * u + c * v - 2.0 * forward(u, 0)
        yv = a1 * v + c * u - 2.0 * forward(v, KL)
        high = [w.astype(BF) for w in (yu, yv)]
        return jnp.concatenate(high + [(w - h.astype(F)).astype(BF) for w, h in zip((yu, yv), high)], 0)

    def stage(tx, yx, G, ys=range(0, CY, 2)):
        for y in ys:
            if tx is not None:
                transpose(tx, y)
                transpose(tx, y + 1)
            if yx is not None:
                left = jnp.concatenate([image(yx, y), image(yx, y + 1)], 1)
                right = jnp.concatenate([m[yx, y], m[yx, y + 1]], 0)
                G = G + jnp.dot(left, right, preferred_element_type=F)
        return G

    x_up = remote(tt.at[3, pl.ds(0, half)], xr.at[0], xsend.at[0], xrecv.at[0], beside["xp"])
    x_down = remote(tt.at[0, pl.ds(half, half)], xr.at[1], xsend.at[1], xrecv.at[1], beside["xm"])
    y_up = remote(tt.at[:, CY - 1], yr.at[0], ysend.at[0], yrecv.at[0], beside["yp"])
    y_down = remote(tt.at[:, 0], yr.at[1], ysend.at[1], yrecv.at[1], beside["ym"])
    z_up = remote(zs.at[1], zr.at[0], zsend.at[0], zrecv.at[0], beside["zp"])
    z_down = remote(zs.at[0], zr.at[1], zsend.at[1], zrecv.at[1], beside["zm"])
    p_up = remote(part.at[1], partr.at[0], psend.at[0], precv.at[0], beside["xp"])
    p_down = remote(part.at[0], partr.at[1], psend.at[1], precv.at[1], beside["xm"])
    ways = [
        ("xp", x_up), ("xm", x_down), ("yp", y_up), ("ym", y_down),
        ("zp", z_up), ("zm", z_down), ("xp", p_up), ("xm", p_down),
    ]

    def start(side, copy):
        @pl.when(has[side])
        def _():
            copy.start()

    def arrived(side, copy, buffer, slot):
        @pl.when(has[side])
        def _():
            copy.wait_recv()

        @pl.when(jnp.logical_not(has[side]))
        def _():
            buffer[slot] = jnp.zeros(buffer.shape[1:], buffer.dtype)

    G = jnp.zeros((4 * KL, 128), F)
    lower_y, upper_y = range(0, half, 2), range(half, CY, 2)
    fetch[3, 0].wait()
    stage(3, None, G, lower_y)

    @pl.when(has["xm"])
    def _():
        pl.semaphore_wait(barrier, peers)
        pl.semaphore_signal(ready, inc=1, device_id=beside["xm"], device_id_type=MESH)

    fetch[0, 1].wait()
    stage(0, None, G, upper_y)
    start("xm", x_down)

    @pl.when(has["xm"] & has["xp"])
    def _():
        pl.semaphore_wait(ready, 1)
        x_up.start()

    fetch[3, 1].wait()
    stage(3, None, G, upper_y)
    fetch[0, 0].wait()
    stage(0, None, G, lower_y)
    fetch[2, None].wait()
    fetch_s.wait()
    G = stage(2, 3, G)

    @pl.when(jnp.logical_not(has["xm"]))
    def _():
        pl.semaphore_wait(barrier, peers)

    fetch[1, None].wait()
    for x in range(CX):
        low = m[x, :, 0:16, :].astype(F)[:, 0, :]
        high = m[x, :, CZ - 16 : CZ, :].astype(F)[:, 15, :]
        ok = live_lanes[:CY]
        zs[0, CY * x : CY * (x + 1)] = jnp.where(ok, low, 0.0).astype(BF)
        zs[1, CY * x : CY * (x + 1)] = jnp.where(ok, high, 0.0).astype(BF)
    start("zp", z_up)
    start("zm", z_down)
    G = stage(1, 2, G)
    start("yp", y_up)
    start("ym", y_down)
    G = stage(None, 1, G)
    G = stage(None, 0, G)
    G = G[: 2 * KL] + G[2 * KL :]

    def both(g):
        return jnp.where(live_lanes[:KL, :KS], g[:KL, :KS] + g[KL : 2 * KL, KS:], 0.0)

    def flip(b):
        wide = jnp.concatenate([b, jnp.zeros((KL, KS), F)], 1)
        wide = jnp.concatenate([wide, jnp.zeros((128 - KL, 128), F)], 0)
        return jnp.transpose(wide)[:KL, :KS]

    C = both(G)
    C = 0.5 * (C + flip(C))
    r48 = lax.broadcasted_iota(jnp.int32, (KL, KS), 0)
    l48 = lax.broadcasted_iota(jnp.int32, (KL, KS), 1)
    C = jnp.where((r48 == l48) & (r48 >= count), 1.0, C)

    def both_z(g):
        return -(g[:KL, :KS] + g[KS : KS + KL, KS:])

    arrived("zm", z_up, zr, 0)
    arrived("zp", z_down, zr, 1)
    zp = both_z(lax.dot_general(zs[1], zr[1], TN, preferred_element_type=F))

    mine = lead.at[jnp.minimum(gz, PSUB - 1)]
    mine_sem = lrecv.at[jnp.minimum(gz, PSUB - 1)]
    along = [remote(mine, mine, lsend.at[t], mine_sem, {"gz": t}) for t in range(PSUB + 1)]

    @pl.when(leader)
    def _():
        lead[jnp.minimum(gz, PSUB - 1)] = jnp.concatenate([C, zp], 1)
        for t in range(PSUB + 1):
            pl.when(gz != t)(along[t].start)

    @pl.when(jnp.logical_not(has["xm"]))
    def _():
        pl.semaphore_wait(ready, 1)
        x_up.start()

    zmT = both_z(lax.dot_general(zr[0], zs[0], TN, preferred_element_type=F))
    zpT = both_z(lax.dot_general(zr[1], zs[1], TN, preferred_element_type=F))

    def face(tiles, own):
        left = jnp.concatenate(tiles, 1)
        right = jnp.concatenate(own, 0)
        return -both(jnp.dot(left, right, preferred_element_type=F))

    arrived("ym", y_up, yr, 0)
    arrived("yp", y_down, yr, 1)
    ymT = face([yr[0, x] for x in range(CX)], [m[x, 0] for x in range(CX)])
    ypT = face([yr[1, x] for x in range(CX)], [m[x, CY - 1] for x in range(CX)])

    def pack(k, a, b):
        gath[gz, k] = jnp.where(core == 1, jnp.concatenate([b, a], 1), jnp.concatenate([a, b], 1))

    zero = jnp.zeros((KL, KS), F)
    pack(0, C, ymT)
    pack(1, ypT, zpT)

    class Gather:
        def __init__(self, at, send, recv, steps):
            give = lambda c, t, k: remote(at(c), at(c), send.at[k], recv.at[c], {"gz": t})
            number = iter(range(15))
            self.steps = [(waits, [give(c, t, next(number)) for c, t in pairs]) for waits, pairs in steps]
            self.sends = [s for _, sends in self.steps for s in sends]
            self.wait = lambda c: remote(at(c), at(c), send.at[0], recv.at[c], {"gz": partner}).wait_recv()

        def step(self, k):
            waits, sends = self.steps[k]
            if len(waits) == len(sends):
                for c, s in zip(waits, sends):
                    self.wait(c)
                    s.start()
                return
            for c in waits:
                self.wait(c)
            for s in sends:
                s.start()

    mine_all = (gz, partner) + around + tuple(also(t) for t in around)
    of_sibling = [t + 1 - 2 * core for t in mine_all]
    far = [also(t) for t in around]
    early = Gather(
        lambda c: gath.at[c, pl.ds(0, 2)], esend, erecv,
        [
            ([], [(gz, t) for t in (partner,) + around + (sibling,)]),
            ([partner], [(partner, t) for t in around + (sibling,)]),
            (list(around), [(t, sibling) for t in around]),
            (far, [(t, sibling) for t in far]),
            (of_sibling, []),
        ],
    )
    late = Gather(
        lambda c: gath.at[c, 2], rsend, rrecv,
        [
            ([], [(gz, t) for t in tuple(far) + around + (partner, sibling)]),
            ([partner] + list(around) + far, [(t, sibling) for t in [partner] + list(around) + far]),
            (of_sibling, []),
        ],
    )
    early.step(0)

    eye = jnp.where(r48 == l48, 1.0, 0.0)
    for i in range(PSUB):
        b = jnp.where(gz == i, C, zero)
        b = jnp.where(gz == i - 1, zpT, b)
        b = jnp.where(gz == i + 1, zmT, b)
        rhs[i] = jnp.concatenate([b, jnp.where(gz == i, eye, zero)], 1)
        xs[i] = jnp.zeros((KL, 128), F)
    sub[...] = jnp.zeros((KL, 256), F)

    r16 = lax.broadcasted_iota(jnp.int32, (KS - KL, NGZ * KS), 0) + KL
    l16 = lax.rem(lax.broadcasted_iota(jnp.int32, (KS - KL, NGZ * KS), 1), KS)
    out[KL:KS, :] = jnp.where(r16 == l16, 1.0, 0.0)
    for b in range(1, 7):
        out[KS * b + KL : KS * (b + 1), :] = jnp.zeros((KS - KL, NGZ * KS), F)

    first_lanes = lax.broadcasted_iota(jnp.int32, (KL, 128), 1) < KS

    def step(i, _):
        @pl.when(gz != i)
        def _():
            remote(lead.at[i], lead.at[i], lsend.at[0], lrecv.at[i], {"gz": partner}).wait_recv()

        g = sub[...]
        a1 = lead[i] - jnp.where(first_lanes, g[:, :128], 0.0)
        a2 = rhs[i] - g[:, 128:]
        A = eliminate([[a1[8 * k : 8 * k + 8], a2[8 * k : 8 * k + 8]] for k in range(KL // 8)])
        a1 = jnp.concatenate([a[0] for a in A], 0)
        a2 = jnp.concatenate([a[1] for a in A], 0)
        xs[i] = a2
        turned = pltpu.roll(a1, KS, 1)
        sub[...] = outer_gram(turned[:, :KS], jnp.concatenate([turned, a2], 1))[:KL]
        return 0

    def chain(low, high):
        @pl.when(chained)
        def _():
            lax.fori_loop(low, high, step, 0)

    early.step(1)
    chain(0, 2)
    early.step(2)
    arrived("xm", x_up, xr, 0)
    low = face([xr[0, y] for y in range(half)], [m[0, y] for y in range(half)])
    part[0] = jnp.concatenate([flip(low), zero], 1)
    start("xm", p_down)
    arrived("xp", x_down, xr, 1)
    high = face([xr[1, y] for y in range(half)], [m[CX - 1, half + y] for y in range(half)])
    part[1] = jnp.concatenate([flip(high), zero], 1)
    start("xp", p_up)
    chain(2, 5)
    arrived("xm", p_up, partr, 0)
    arrived("xp", p_down, partr, 1)
    xpT = high + partr[1, :, :KS]
    pack(2, low + partr[0, :, :KS], xpT)
    late.step(0)
    early.step(3)
    chain(5, PSUB)

    to_y = remote(post.at[0], postr, osend.at[0], orecv, beside["yp"])
    to_x = remote(post.at[1], postr, osend.at[1], orecv, beside["xp"])

    @pl.when(leader)
    def _():
        right = jnp.concatenate([flip(ypT), flip(xpT)], 1)
        wide = [
            jnp.dot(xs[i][:, KS : KS + KL], right, precision=lax.Precision.HIGHEST, preferred_element_type=F)
            for i in range(PSUB)
        ]
        for p in range(PSUB // 2):
            a, b = wide[2 * p], wide[2 * p + 1]
            post[0, p] = jnp.concatenate([a[:, :KS], b[:, :KS]], 1)
            post[1, p] = jnp.concatenate([a[:, KS:], b[:, KS:]], 1)
        to_y.start()
        to_x.start()


    @pl.when(chained)
    def _():
        late.step(1)

    left = lax.broadcasted_iota(jnp.int32, (KL, 128), 1) < KS

    def lay(p, k, a, b):
        first, second = gath[2 * p, k], gath[2 * p + 1, k]
        cols = slice(128 * p, 128 * (p + 1))
        out[KS * a : KS * a + KL, cols] = jnp.where(left, first, second)
        out[KS * b : KS * b + KL, cols] = pltpu.roll(jnp.where(left, second, first), KS, 1)

    early.step(4)
    for p in range(NGZ // 2):
        lay(p, 0, 0, 3)
        lay(p, 1, 4, 6)
        below = gath[2 * p - 1, 1] if p > 0 else jnp.zeros((KL, 128), F)
        both_below = jnp.where(left, below, gath[2 * p, 1])
        turned = jnp.transpose(jnp.concatenate([both_below, jnp.zeros((128 - KL, 128), F)], 0))
        out[KS * 5 : KS * 5 + KL, 128 * p : 128 * (p + 1)] = jnp.concatenate(
            [turned[:KL, :KS], turned[KS : KS + KL, :KS]], 1
        )

    def put_panel(p, tile, ends):
        t = jnp.transpose(jnp.concatenate([tile, jnp.zeros((128 - KL, 128), F)], 0))
        panel_ref[:, 128 * p : 128 * (p + 1)] = jnp.concatenate([t[:KS, :KS], t[KS:, :KS]], 1) + ends

    panel_ref[...] = jnp.zeros((KS, PSUB * KS), F)

    @pl.when(chained)
    def _():
        r64 = lax.broadcasted_iota(jnp.int32, (KS, KS), 0)
        l64 = lax.broadcasted_iota(jnp.int32, (KS, KS), 1)
        dead = jnp.where((r64 == l64) & (r64 >= KL), 1.0, 0.0)
        for p in range(PSUB // 2):
            ends = [jnp.where(gz == 2 * p + k, dead, jnp.zeros((KS, KS), F)) for k in range(2)]
            tile = jnp.concatenate([xs[2 * p][:, :KS], xs[2 * p + 1][:, :KS]], 1)
            put_panel(p, tile, jnp.concatenate(ends, 1))

    @pl.when(jnp.logical_not(chained))
    def _():
        late.step(1)

    late.step(2)
    for p in range(NGZ // 2):
        lay(p, 2, 1, 2)

    @pl.when(follower)
    def _():
        to_y.wait_recv()
        for p in range(PSUB // 2):
            put_panel(p, postr[p], 0.0)

    for s in early.sends + late.sends:
        s.wait_send()
    for side, copy in ways:
        @pl.when(has[side])
        def _():
            copy.wait_send()

    @pl.when(leader)
    def _():
        to_y.wait_send()
        to_x.wait_send()
        for t in range(PSUB + 1):
            pl.when(gz != t)(along[t].wait_send)


def local(vectors, diag_shift, coupling, counts):
    dma = pltpu.SemaphoreType.DMA
    columns, panel = pl.pallas_call(
        kernel,
        out_shape=(
            jax.ShapeDtypeStruct((7 * KS, NGZ * KS), F),
            jax.ShapeDtypeStruct((KS, PSUB * KS), F),
        ),
        in_specs=[pl.BlockSpec(memory_space=pltpu.SMEM)] + [pl.BlockSpec(memory_space=pltpu.HBM)] * 2,
        out_specs=(pl.BlockSpec(memory_space=pltpu.VMEM), pl.BlockSpec(memory_space=pltpu.VMEM)),
        scratch_shapes=[
            pltpu.VMEM((CX, CY, CZ, 128), BF),
            pltpu.VMEM((CX, CY, 2 * KL, CZ), BF),
            pltpu.VMEM((3, CX, CY, CZ), F),
            pltpu.VMEM((2, CY // 2, 2 * KL, CZ), BF),
            pltpu.VMEM((2, CX, 2 * KL, CZ), BF),
            pltpu.VMEM((2, CX * CY, 128), BF),
            pltpu.VMEM((2, CX * CY, 128), BF),
            pltpu.VMEM((2, KL, 128), F),
            pltpu.VMEM((2, KL, 128), F),
            pltpu.VMEM((PSUB, KL, 128), F),
            pltpu.VMEM((PSUB, KL, 128), F),
            pltpu.VMEM((PSUB, KL, 128), F),
            pltpu.VMEM((KL, 256), F),
            pltpu.VMEM((NGZ, 3, KL, 128), F),
            pltpu.VMEM((2, PSUB // 2, KL, 128), F),
            pltpu.VMEM((PSUB // 2, KL, 128), F),
            pltpu.SemaphoreType.REGULAR,
            dma((7,)),
            dma((2,)), dma((2,)), dma((2,)), dma((2,)), dma((2,)), dma((2,)), dma((2,)), dma((2,)),
            dma((PSUB + 1,)), dma((PSUB,)), dma((2,)), dma, dma((15,)), dma((NGZ,)), dma((15,)), dma((NGZ,)),
        ],
        compiler_params=pltpu.CompilerParams(
            collective_id=0, has_side_effects=True, vmem_limit_bytes=(50 << 20) + (100 << 10)
        ),
    )(counts, vectors, jnp.concatenate([diag_shift, coupling[None]], 0))
    return columns.T, panel


def solution(mesh):
    return jax.shard_map(
        local,
        mesh=mesh,
        in_specs=(
            P("gx", "gy", "gz", None),
            P(None, "gx", "gy", "gz"),
            P("gx", "gy", "gz"),
            P(("gx", "gy", "gz")),
        ),
        out_specs=(P(("gx", "gy"), None), P(("gx", "gy", "gz"), None)),
        check_vma=False,
    )
```
